256 devices in a mesh: ctx: 32 (over y, z_lo, x), tp: 8 (over z_hi, core).
Axes of the slice: x: 4, y: 4, z: 8 (z_hi: 4, z_lo: 2; z = z_hi * 2 + z_lo), core: 2. Of those that a mesh axis runs over, the one named last changes fastest.
Arguments:
- tokens: bfloat16 [8192, 4096], P('ctx', 'tp'), may hold values from -6 to 6
- norm_gain: bfloat16 [4096], replicated, may hold values from 0.5 to 1.5
- w_query: bfloat16 [4096, 4096], P(None, 'tp'), may hold values from -2 to 2
- w_key: bfloat16 [4096, 1024], P(None, 'tp'), may hold values from -6 to 6
- w_value: bfloat16 [4096, 1024], P(None, 'tp'), may hold values from -0.09375 to 0.09375
- w_output: bfloat16 [4096, 4096], P('tp'), may hold values from -0.375 to 0.375
Outputs:
- update: bfloat16 [8192, 4096], P('ctx', 'tp')
The draws below stay inside these ranges and needn't reach their ends.
All inputs are finite; a program needn't handle non-finite values.
Results may differ from the reference program's by a relative error of at most 0.02.
The reference program's roundings to bfloat16 on the way count: a program that leaves them out, or rounds other values in their place, can miss the bound.
Values may be sent and summed in bfloat16 or wider, within the bound.
A program may use at most 64 MiB of HBM per device.

```python
import jax
import jax.numpy as jnp
from jax import lax

D = 4096
HEADS = 32
KV_HEADS = 8
HEAD_DIM = 128
SEQ = 8192
N_TP = 8


def shared_query(key):
    return jnp.clip(jax.random.normal(key, (D, HEADS * HEAD_DIM), jnp.float32), -4.0, 4.0)


def draw_w_query(key, part):
    base = shared_query(key)
    return (base * (4.0 / D) ** 0.5).astype(jnp.bfloat16)


def draw_w_key(key, part):
    key = jax.random.fold_in(key, 7)
    fresh = jnp.clip(jax.random.normal(key, (D, KV_HEADS * HEAD_DIM), jnp.float32), -4.0, 4.0) * (1.0 / D) ** 0.5
    return fresh.astype(jnp.bfloat16)


def block_levels(key, shape, cuts, smallest, top_value):
    factor_of, own = 1.0, jax.random.fold_in(key, 6)
    for axis_at, blocks in cuts:
        draws = jnp.exp(jax.random.uniform(jax.random.fold_in(own, axis_at), (blocks,), jnp.float32, smallest / len(cuts), top_value / len(cuts)))
        factor_of = factor_of * jnp.repeat(draws, shape[axis_at] // blocks).reshape([-1 if axis == axis_at else 1 for axis in range(len(shape))])
    return factor_of


def bell_draw(rng, dims, deviation, reach, shards=(), kind=jnp.bfloat16):
    entries = jax.random.normal(rng, dims, jnp.float32) * deviation
    if len(shards) > 0:
        entries = block_levels(rng, dims, shards, -0.22, 0.18) * entries
    return jnp.clip(entries, min=-reach, max=reach).astype(kind)


def setup_inputs(seed: int = 0) -> dict:
    splits = jax.random.split(jax.random.key(seed), 7)
    return {
        "tokens": bell_draw(splits[0], (SEQ, D), 1.0, 6.0, ((0, 32), (1, 8))),
        "norm_gain": jnp.clip(1.0 + 0.1 * jax.random.normal(splits[1], (D,), jnp.float32), 0.5, 1.5).astype(jnp.bfloat16),
        "w_query": draw_w_query(jax.random.fold_in(splits[6], 71), 0),
        "w_key": draw_w_key(jax.random.fold_in(splits[6], 71), 0),
        "w_value": bell_draw(splits[4], (D, KV_HEADS * HEAD_DIM), D ** -0.5, 0.09375, ((1, 8),)),
        "w_output": bell_draw(splits[5], (HEADS * HEAD_DIM, D), (D // 16) ** -0.5, 0.375, ((0, 8),)),
    }


def rotate(field, positions):
    half_dim = field.shape[-1] // 2
    frequency = 500000.0 ** (-2.0 * jnp.arange(half_dim, dtype=jnp.float32) / (2 * half_dim))
    angles = positions.astype(jnp.float32)[:, None] * frequency[None, :]
    cosine = jnp.cos(angles)
    sine = jnp.sin(angles)
    first = field[..., :half_dim]
    second = field[..., half_dim:]
    return jnp.concatenate([first * cosine - second * sine, second * cosine + first * sine], axis=-1)

def reference(tokens, norm_gain, w_query, w_key, w_value, w_output):
    widened = tokens.astype(jnp.float32)
    normed = (widened * lax.rsqrt(lax.optimization_barrier(jnp.mean(widened * widened, axis=-1, keepdims=True)) + 1e-05) * norm_gain.astype(jnp.float32)).astype(jnp.bfloat16)
    positions = jnp.arange(SEQ, dtype=jnp.int32)
    query = jnp.dot(normed, w_query, preferred_element_type=jnp.float32).reshape(SEQ, HEADS, HEAD_DIM)
    query = rotate(jnp.transpose(query, (1, 0, 2)), positions).astype(jnp.bfloat16)
    key_rows = jnp.dot(normed, w_key, preferred_element_type=jnp.float32).reshape(SEQ, KV_HEADS, HEAD_DIM)
    key_rows = rotate(jnp.transpose(key_rows, (1, 0, 2)), positions).astype(jnp.bfloat16)
    value_rows = jnp.dot(normed, w_value, preferred_element_type=jnp.float32).reshape(SEQ, KV_HEADS, HEAD_DIM)
    value_rows = jnp.transpose(value_rows, (1, 0, 2)).astype(jnp.bfloat16)
    group_size = HEADS // KV_HEADS
    score_scale = 1.0 / HEAD_DIM ** 0.5
    causal = positions[None, :] <= positions[:, None]

    def one_head(head_index):
        head_query = query[head_index]
        head_keys = key_rows[head_index // group_size]
        head_values = value_rows[head_index // group_size]
        scores = jnp.dot(head_query, head_keys.T, preferred_element_type=jnp.float32) * score_scale
        scores = jnp.where(causal, scores, -1e+30)
        row_max = lax.optimization_barrier(jnp.max(scores, axis=-1, keepdims=True))
        weights = jnp.where(causal, jnp.exp(scores - row_max), 0.0)
        denominator = lax.optimization_barrier(jnp.sum(weights, axis=-1))
        summed = jnp.dot(weights.astype(jnp.bfloat16), head_values, preferred_element_type=jnp.float32)
        return (summed / denominator[:, None]).astype(jnp.bfloat16)
    attention = lax.map(one_head, jnp.arange(HEADS, dtype=jnp.int32))
    heads_part = HEADS // N_TP
    update = jnp.zeros((SEQ, D), jnp.float32)
    for group_index in range(N_TP):
        chosen = attention[group_index * heads_part:(group_index + 1) * heads_part].astype(jnp.float32)
        rows_part = w_output[group_index * heads_part * HEAD_DIM:(group_index + 1) * heads_part * HEAD_DIM]
        rows_part = rows_part.reshape(heads_part, HEAD_DIM, D).astype(jnp.float32)
        group_term = jnp.einsum('htk,hkd->td', chosen, rows_part)
        rounded = lax.optimization_barrier(group_term.astype(jnp.bfloat16))
        update = update + rounded.astype(jnp.float32)
    return update.astype(jnp.bfloat16)
```

```python
import functools

import jax
import jax.numpy as jnp
from jax import lax
from jax.experimental import pallas as pl
from jax.experimental.pallas import tpu as pltpu
from jax.sharding import PartitionSpec as P

HEAD_DIM = 128
MESH = pl.DeviceIdType.MESH
ROWS = 256
HALF = 128
WIDTH = 4096
NC = 8
R = ROWS // NC
NS = 26
ND = 4
CR = ROWS // ND
MS = 6
CHUNK_KEYS = 8 * R
LOG2E = 1.4426950408889634


def device_at(x, y, z_hi, z_lo, core):
    return ((y % 4) * 8 + z_lo * 4 + x % 4, (z_hi % 4) * 2 + core)


def sublayer(
    tok, gain, cosine, sine, wq, wk, wv, wo, out,
    gathered, wqkv, wov, kv, q_here, q_away, top, denom, acc, att,
    term_away, term_in, term_own, relay_out, relay_in, fin_out, fin_in, back,
    w_sem, c_send, c_recv, d_send, d_recv,
):
    ctx = lax.axis_index("ctx")
    tp = lax.axis_index("tp")
    x, y, z_lo = ctx % 4, ctx // 8, (ctx // 4) % 2
    z_hi, core = tp // 2, tp % 2
    z_up = device_at(x, y, z_hi + 1, z_lo, core)
    z_down = device_at(x, y, z_hi + 3, z_lo, core)
    sibling = device_at(x, y, z_hi, z_lo, 1 - core)
    z_pair = device_at(x, y, z_hi, 1 - z_lo, core)
    x_up = device_at(x + 1, y, z_hi, z_lo, core)
    x_down = device_at(x + 3, y, z_hi, z_lo, core)
    y_up = device_at(x, y + 1, z_hi, z_lo, core)
    y_down = device_at(x, y + 3, z_hi, z_lo, core)
    partner = device_at(x, 3 - y, z_hi, z_lo, core)

    weights = [
        pltpu.make_async_copy(wq, wqkv.at[:, pl.ds(0, 512)], w_sem.at[0]),
        pltpu.make_async_copy(wk, wqkv.at[:, pl.ds(512, 128)], w_sem.at[1]),
        pltpu.make_async_copy(wv, wqkv.at[:, pl.ds(640, 128)], w_sem.at[2]),
        pltpu.make_async_copy(wo, wov, w_sem.at[3]),
    ]
    for copy in weights:
        copy.start()
    gathered[tp] = tok[...]

    barrier = pltpu.get_barrier_semaphore()
    peers = (z_up, z_down, sibling, z_pair, x_up, x_down, y_up, y_down)
    for peer in peers:
        pl.semaphore_signal(barrier, inc=1, device_id=peer, device_id_type=MESH)
    pl.semaphore_wait(barrier, len(peers))

    x_lo, x_hi, y_lo, y_hi = (x + 3) % 4, (x + 1) % 4, (y + 3) % 4, (y + 1) % 4

    def copy_c(number, c):
        rows = pl.ds(pl.multiple_of(c * R, R), R)
        first = pl.ds(pl.multiple_of(c * R, R // 2), R // 2)
        second = pl.ds(pl.multiple_of(c * R + R // 2, R // 2), R // 2)
        places = [
            lambda: (gathered.at[tp, rows], z_up),
            lambda: (gathered.at[tp, rows], z_down),
            lambda: (gathered.at[tp, rows], sibling),
            lambda: (gathered.at[(tp + 6) % 8, first], z_up),
            lambda: (gathered.at[(tp + 2) % 8, second], z_down),
            lambda: (gathered.at[(tp + 6) % 8, rows], sibling),
            lambda: (gathered.at[(tp + 2) % 8, rows], sibling),
            lambda: (gathered.at[(tp + 4) % 8, rows], sibling),
            lambda: (kv.at[:, c, y, x, z_lo], z_pair),
            lambda: (kv.at[0, c, y, x], x_up),
            lambda: (kv.at[0, c, y, x], x_down),
            lambda: (kv.at[0, c, y, x_lo, 0], x_up),
            lambda: (kv.at[0, c, y, x_hi, 1], x_down),
            lambda: (kv.at[0, c, y], y_up),
            lambda: (kv.at[0, c, y], y_down),
            lambda: (kv.at[0, c, y_lo, pl.ds(0, 2)], y_up),
            lambda: (kv.at[0, c, y_hi, pl.ds(2, 2)], y_down),
            lambda: (kv.at[1, c, y, x], y_up),
            lambda: (kv.at[1, c, y, x], y_down),
            lambda: (kv.at[1, c, y_lo, x, 0], y_up),
            lambda: (kv.at[1, c, y_hi, x, 1], y_down),
            lambda: (kv.at[1, c, :, x], x_up),
            lambda: (kv.at[1, c, :, x], x_down),
            lambda: (kv.at[1, c, pl.ds(0, 2), x_lo], x_up),
            lambda: (kv.at[1, c, pl.ds(2, 2), x_hi], x_down),
        ]
        if number < 25:
            place, target = places[number]()
            source = place
        else:
            rest = pl.ds(pl.multiple_of((c - NC // 2) * R, R), R)
            source, place, target = q_away.at[:, rest], q_here.at[0, :, rest], partner
        return pltpu.make_async_remote_copy(
            src_ref=source, dst_ref=place, send_sem=c_send.at[c, number], recv_sem=c_recv.at[c, number],
            device_id=target, device_id_type=MESH,
        )

    def start(numbers, c):
        for number in numbers:
            copy_c(number, c).start()

    def arrive(numbers, c):
        for number in numbers:
            copy_c(number, c).wait_recv()

    def rotate(field, cos_rows, sin_rows):
        return field * cos_rows + pltpu.roll(field, HEAD_DIM // 2, 1) * sin_rows

    def project(c):
        rows = pl.ds(pl.multiple_of(c * R, R), R)
        squares = jnp.zeros((R, 512), jnp.float32)
        for piece in range(8):
            values = gathered[piece, rows].astype(jnp.float32)
            squares = squares + values * values
        scale = lax.rsqrt(jnp.sum(squares, axis=1, keepdims=True) * (1.0 / WIDTH) + 1e-05)
        total = jnp.zeros((R, 768), jnp.float32)
        for piece in range(8):
            values = gathered[piece, rows].astype(jnp.float32)
            normed = (values * scale * gain[:, piece * 512:(piece + 1) * 512].astype(jnp.float32)).astype(jnp.bfloat16)
            total = total + jnp.dot(
                normed, wqkv[piece * 512:(piece + 1) * 512, :], preferred_element_type=jnp.float32
            )
        cos_rows, sin_rows = cosine[rows], sine[rows]
        kv[0, c, y, x, z_lo] = rotate(total[:, 512:640], cos_rows, sin_rows).astype(jnp.bfloat16)
        kv[1, c, y, x, z_lo] = total[:, 640:768].astype(jnp.bfloat16)
        queries = [
            rotate(total[:, h * 128:(h + 1) * 128], cos_rows, sin_rows).astype(jnp.bfloat16) for h in range(4)
        ]

        @pl.when(c < NC // 2)
        def _():
            for h in range(4):
                q_here[1, h, rows] = queries[h]

        @pl.when(c >= NC // 2)
        def _():
            rest = pl.ds(pl.multiple_of((c - NC // 2) * R, R), R)
            for h in range(4):
                q_away[h, rest] = queries[h]

    top[...] = jnp.full(top.shape, -1e30, jnp.float32)
    denom[...] = jnp.zeros(denom.shape, jnp.float32)
    acc[...] = jnp.zeros(acc.shape, jnp.float32)
    factor_log = LOG2E / HEAD_DIM ** 0.5

    def fold(c, half, group, masked):
        keys = kv[0, c, group].reshape(CHUNK_KEYS, HEAD_DIM)
        values = kv[1, c, group].reshape(CHUNK_KEYS, HEAD_DIM)
        queries = q_here[half].reshape(4 * HALF, HEAD_DIM)
        scores = lax.dot_general(
            queries, keys, (((1,), (1,)), ((), ())), preferred_element_type=jnp.float32
        )
        if masked:
            row = lax.broadcasted_iota(jnp.int32, (4 * HALF, 1), 0) % HALF + (1 - half) * HALF
            column = lax.broadcasted_iota(jnp.int32, (1, CHUNK_KEYS), 1)
            block = (column // R) % 2 * 4 + column // (2 * R)
            key_row = (block - (z_lo * 4 + x)) * ROWS + c * R + column % R
            scores = jnp.where(key_row <= row, scores, -2e30)
        old = top[half]
        newest = jnp.maximum(old, jnp.max(scores, axis=1, keepdims=True))
        top[half] = newest
        shrink = jnp.exp2((old - newest) * factor_log)
        wide = jnp.concatenate([newest] * (CHUNK_KEYS // 128), axis=1)
        weights = jnp.exp2((scores - wide) * factor_log)
        part = weights[:, 0:128]
        for at in range(1, CHUNK_KEYS // 128):
            part = part + weights[:, at * 128:(at + 1) * 128]
        denom[half] = denom[half] * shrink + part
        acc[half] = acc[half] * shrink + jnp.dot(
            weights.astype(jnp.bfloat16), values, preferred_element_type=jnp.float32
        )

    def attend(c):
        groups_away = 3 - y

        def body(step, carry):
            half = (step >= groups_away).astype(jnp.int32)
            group = step - half * groups_away
            fold(c, half, group, False)
            return carry

        lax.fori_loop(0, 3, body, 0)

        def diagonal(half, carry):
            fold(c, half, jnp.where(half == 0, 3 - y, y), True)
            return carry

        lax.fori_loop(0, 2, diagonal, 0)

    start((0, 1, 2), 0)
    start((0, 1, 2), 1)

    def tick(t, carry):
        @pl.when((t >= 5) & (t < NC + 5))
        def _():
            arrive((13, 14), t - 5)
            start((15, 16), t - 5)
            arrive((21, 22), t - 5)
            start((23, 24), t - 5)

        @pl.when((t >= 4) & (t < NC + 4))
        def _():
            arrive((11, 12), t - 4)
            start((13, 14), t - 4)
            arrive((19, 20), t - 4)
            start((21, 22), t - 4)

        @pl.when((t >= 3) & (t < NC + 3))
        def _():
            arrive((9, 10), t - 3)
            start((11, 12), t - 3)
            arrive((17, 18), t - 3)
            start((19, 20), t - 3)

        @pl.when((t >= 2) & (t < NC + 2))
        def _():
            arrive((8,), t - 2)
            start((9, 10, 17, 18), t - 2)

        @pl.when(t < NC)
        def _():
            arrive((0, 1), t)
            start((3, 4, 5, 6), t)

        @pl.when(t + 2 < NC)
        def _():
            start((0, 1, 2), t + 2)

        @pl.when(t == 1)
        def _():
            for copy in weights[:3]:
                copy.wait()

        @pl.when((t >= 1) & (t < NC + 1))
        def _():
            arrive((2, 5, 6, 7), t - 1)
            project(t - 1)
            start((8,), t - 1)

        @pl.when((t >= NC // 2 + 1) & (t < NC + 1))
        def _():
            start((25,), t - 1)

        @pl.when(t < NC)
        def _():
            arrive((3, 4), t)
            start((7,), t)

        @pl.when(t == NC)
        def _():
            for c in range(NC // 2, NC):
                arrive((25,), c)

        @pl.when(t >= NC)
        def _():
            arrive((15, 16, 23, 24), t - NC)
            attend(t - NC)

        return carry

    lax.fori_loop(0, 2 * NC, tick, 0)

    for half in range(2):
        whole = acc[half] / jnp.sum(denom[half], axis=1, keepdims=True)
        for h in range(4):
            att[half * HALF:(half + 1) * HALF, h * 128:(h + 1) * 128] = whole[
                h * HALF:(h + 1) * HALF
            ].astype(jnp.bfloat16)
    weights[3].wait()

    def copy_d(number, u):
        return pltpu.make_async_remote_copy(
            **dict(zip(("src_ref", "dst_ref", "device_id"), (
                lambda: (term_away.at[u], term_in.at[u], sibling),
                lambda: (relay_out.at[0, u], relay_in.at[0, u], z_up),
                lambda: (relay_out.at[1, u], relay_in.at[1, u], z_down),
                lambda: (fin_out.at[0, u], fin_in.at[0, u], z_up),
                lambda: (fin_out.at[1, u], fin_in.at[1, u], z_down),
                lambda: (
                    back.at[pl.ds(pl.multiple_of(u * CR, CR), CR)],
                    out.at[pl.ds(pl.multiple_of(HALF + u * CR, CR), CR)],
                    partner,
                ),
            )[number]())),
            send_sem=d_send.at[u, number], recv_sem=d_recv.at[u, number], device_id_type=MESH,
        )

    def term(u, column):
        return jnp.dot(
            att[pl.ds(pl.multiple_of(u * CR, CR), CR)],
            wov[:, pl.ds(pl.multiple_of(column * 512, 512), 512)],
            preferred_element_type=jnp.float32,
        ).astype(jnp.bfloat16)

    def paired(u, at, rows):
        return term_own[u, at, rows].astype(jnp.float32) + term_in[u, at, rows].astype(jnp.float32)

    low, high = pl.ds(0, CR // 2), pl.ds(CR // 2, CR // 2)
    opposite, above, below = (z_hi + 2) % 4, (z_hi + 1) % 4, (z_hi + 3) % 4

    def out_tick(u, carry):
        @pl.when(u < ND)
        def _():
            for at in range(4):
                term_away[u, at] = term(u, at * 2 + 1 - core)
            copy_d(0, u).start()
            for at in range(4):
                term_own[u, at] = term(u, at * 2 + core)
            copy_d(0, u).wait_recv()
            relay_out[0, u] = paired(u, opposite, low).astype(jnp.bfloat16)
            copy_d(1, u).start()
            relay_out[1, u] = paired(u, opposite, high).astype(jnp.bfloat16)
            copy_d(2, u).start()

        @pl.when((u >= 1) & (u < ND + 1))
        def _():
            v = u - 1
            copy_d(1, v).wait_recv()
            fin_out[0, v, low] = (paired(v, above, low) + relay_in[0, v].astype(jnp.float32)).astype(jnp.bfloat16)
            fin_out[0, v, high] = paired(v, above, high).astype(jnp.bfloat16)
            copy_d(3, v).start()
            copy_d(2, v).wait_recv()
            fin_out[1, v, low] = paired(v, below, low).astype(jnp.bfloat16)
            fin_out[1, v, high] = (paired(v, below, high) + relay_in[1, v].astype(jnp.float32)).astype(jnp.bfloat16)
            copy_d(4, v).start()

        @pl.when(u >= 2)
        def _():
            v = u - 2
            copy_d(3, v).wait_recv()
            copy_d(4, v).wait_recv()
            whole = (
                paired(v, z_hi, pl.ds(0, CR)) + fin_in[0, v].astype(jnp.float32) + fin_in[1, v].astype(jnp.float32)
            ).astype(jnp.bfloat16)

            @pl.when(v < ND // 2)
            def _():
                back[pl.ds(pl.multiple_of(v * CR, CR), CR)] = whole
                copy_d(5, v).start()

            @pl.when(v >= ND // 2)
            def _():
                out[pl.ds(pl.multiple_of(v * CR - HALF, CR), CR)] = whole

        return carry

    lax.fori_loop(0, ND + 2, out_tick, 0)

    def drain_c(c, carry):
        for number in range(25):
            copy_c(number, c).wait_send()
        return carry

    def drain_q(c, carry):
        copy_c(25, c).wait_send()
        return carry

    def drain_d(u, carry):
        for number in range(5):
            copy_d(number, u).wait_send()
        return carry

    def drain_y(u, carry):
        copy_d(5, u).wait()
        return carry

    lax.fori_loop(0, NC, drain_c, 0)
    lax.fori_loop(NC // 2, NC, drain_q, 0)
    lax.fori_loop(0, ND, drain_d, 0)
    lax.fori_loop(0, ND // 2, drain_y, 0)


def body(tokens, norm_gain, w_query, w_key, w_value, w_output):
    half = HEAD_DIM // 2
    frequency = 500000.0 ** (-2.0 * jnp.arange(half, dtype=jnp.float32) / HEAD_DIM)
    positions = lax.axis_index("ctx") * ROWS + jnp.arange(ROWS, dtype=jnp.int32)
    angles = positions.astype(jnp.float32)[:, None] * frequency[None, :]
    cosine = jnp.cos(angles)
    sine = jnp.sin(angles)
    cosine = jnp.concatenate([cosine, cosine], axis=1)
    sine = jnp.concatenate([-sine, sine], axis=1)
    vmem = pl.BlockSpec(memory_space=pltpu.VMEM)
    hbm = pl.BlockSpec(memory_space=pl.ANY)
    bf16, f32 = jnp.bfloat16, jnp.float32
    return pl.pallas_call(
        sublayer,
        out_shape=jax.ShapeDtypeStruct((ROWS, 512), bf16),
        in_specs=[vmem] * 4 + [hbm] * 4,
        out_specs=vmem,
        scratch_shapes=[
            pltpu.VMEM((8, ROWS, 512), bf16),
            pltpu.VMEM((WIDTH, 768), bf16),
            pltpu.VMEM((512, WIDTH), bf16),
            pltpu.VMEM((2, NC, 4, 4, 2, R, HEAD_DIM), bf16),
            pltpu.VMEM((2, 4, HALF, HEAD_DIM), bf16),
            pltpu.VMEM((4, HALF, HEAD_DIM), bf16),
            pltpu.VMEM((2, 4 * HALF, 128), f32),
            pltpu.VMEM((2, 4 * HALF, 128), f32),
            pltpu.VMEM((2, 4 * HALF, HEAD_DIM), f32),
            pltpu.VMEM((ROWS, 512), bf16),
            pltpu.VMEM((ND, 4, CR, 512), bf16),
            pltpu.VMEM((ND, 4, CR, 512), bf16),
            pltpu.VMEM((ND, 4, CR, 512), bf16),
            pltpu.VMEM((2, ND, CR // 2, 512), bf16),
            pltpu.VMEM((2, ND, CR // 2, 512), bf16),
            pltpu.VMEM((2, ND, CR, 512), bf16),
            pltpu.VMEM((2, ND, CR, 512), bf16),
            pltpu.VMEM((HALF, 512), bf16),
            pltpu.SemaphoreType.DMA((4,)),
            pltpu.SemaphoreType.DMA((NC, NS)),
            pltpu.SemaphoreType.DMA((NC, NS)),
            pltpu.SemaphoreType.DMA((ND, MS)),
            pltpu.SemaphoreType.DMA((ND, MS)),
        ],
        compiler_params=pltpu.CompilerParams(
            collective_id=0, has_side_effects=True, vmem_limit_bytes=52 << 20
        ),
        cost_estimate=pl.CostEstimate(flops=6_000_000_000, bytes_accessed=12_000_000, transcendentals=6_000_000),
    )(tokens, norm_gain.reshape(1, WIDTH), cosine, sine, w_query, w_key, w_value, w_output)


def solution(mesh):
    placed = (P("ctx", "tp"), P(), P(None, "tp"), P(None, "tp"), P(None, "tp"), P("tp", None))
    return jax.shard_map(
        body, mesh=mesh, in_specs=placed, out_specs=P("ctx", "tp"), check_vma=False
    )
```

```python
import functools

import jax
import jax.numpy as jnp
from jax import lax
from jax.experimental import pallas as pl
from jax.experimental.pallas import tpu as pltpu
from jax.sharding import PartitionSpec as P

HEAD_DIM = 128
MESH = pl.DeviceIdType.MESH
ROWS = 256
HALF = 128
WIDTH = 4096
NC = 4
R = ROWS // NC
NS = 26
ND = 4
CR = ROWS // ND
MS = 6
AHEAD = 3
A_DIRECT, P1_DIRECT, P2_DIRECT = False, False, False
LAG_A3, LAG_P, LAG_S1, LAG_S2, LAG_S3, LAG_S4, LAG_ATT = 2, 3, 5, 7, 9, 11, 13
LAG_D3, LAG_D4 = 1, 3
CHUNK_KEYS = 8 * R
LOG2E = 1.4426950408889634


def device_at(x, y, z_hi, z_lo, core):
    return ((y % 4) * 8 + z_lo * 4 + x % 4, (z_hi % 4) * 2 + core)


def sublayer(
    tok, gain, cosine, sine, wq, wk, wv, wo, out,
    gathered, wqkv, wov, kv, q_here, q_away, top, denom, acc, att,
    term_away, term_in, term_own, relay_out, relay_in, fin_out, fin_in, back,
    w_sem, c_send, c_recv, d_send, d_recv,
):
    ctx = lax.axis_index("ctx")
    tp = lax.axis_index("tp")
    x, y, z_lo = ctx % 4, ctx // 8, (ctx // 4) % 2
    z_hi, core = tp // 2, tp % 2
    z_up = device_at(x, y, z_hi + 1, z_lo, core)
    z_down = device_at(x, y, z_hi + 3, z_lo, core)
    sibling = device_at(x, y, z_hi, z_lo, 1 - core)
    z_pair = device_at(x, y, z_hi, 1 - z_lo, core)
    x_up = device_at(x + 1, y, z_hi, z_lo, core)
    x_down = device_at(x + 3, y, z_hi, z_lo, core)
    y_up = device_at(x, y + 1, z_hi, z_lo, core)
    y_down = device_at(x, y + 3, z_hi, z_lo, core)
    partner = device_at(x, 3 - y, z_hi, z_lo, core)

    weights = [
        pltpu.make_async_copy(wq, wqkv.at[:, pl.ds(0, 512)], w_sem.at[0]),
        pltpu.make_async_copy(wk, wqkv.at[:, pl.ds(512, 128)], w_sem.at[1]),
        pltpu.make_async_copy(wv, wqkv.at[:, pl.ds(640, 128)], w_sem.at[2]),
        pltpu.make_async_copy(wo, wov, w_sem.at[3]),
    ]
    own_tokens = pltpu.make_async_copy(tok, gathered.at[tp], w_sem.at[4])
    own_tokens.start()
    for copy in weights:
        copy.start()

    barrier = pltpu.get_barrier_semaphore()
    peers = (z_up, z_down, sibling, z_pair, x_up, x_down, y_up, y_down)
    for peer in peers:
        pl.semaphore_signal(barrier, inc=1, device_id=peer, device_id_type=MESH)
    own_tokens.wait()
    pl.semaphore_wait(barrier, len(peers))

    x_lo, x_hi, y_lo, y_hi = (x + 3) % 4, (x + 1) % 4, (y + 3) % 4, (y + 1) % 4

    def copy_c(number, c):
        rows = pl.ds(pl.multiple_of(c * R, R), R)
        first = pl.ds(pl.multiple_of(c * R, R // 2), R // 2)
        second = pl.ds(pl.multiple_of(c * R + R // 2, R // 2), R // 2)
        x_far = device_at(x + 2, y, z_hi, z_lo, core)
        y_far = device_at(x, y + 2, z_hi, z_lo, core)
        z_far = device_at(x, y, z_hi + 2, z_lo, core)
        places = [
            lambda: (gathered.at[tp, rows], z_up),
            lambda: (gathered.at[tp, rows], z_down),
            lambda: (gathered.at[tp, rows], sibling),
            (lambda: (gathered.at[tp, rows], z_far)) if A_DIRECT
            else (lambda: (gathered.at[(tp + 6) % 8, first], z_up)),
            lambda: (gathered.at[(tp + 2) % 8, second], z_down),
            lambda: (gathered.at[(tp + 6) % 8, rows], sibling),
            lambda: (gathered.at[(tp + 2) % 8, rows], sibling),
            lambda: (gathered.at[(tp + 4) % 8, rows], sibling),
            lambda: (kv.at[:, c, y, x, z_lo], z_pair),
            lambda: (kv.at[0, c, y, x], x_up),
            lambda: (kv.at[0, c, y, x], x_down),
            (lambda: (kv.at[0, c, y, x], x_far)) if P1_DIRECT
            else (lambda: (kv.at[0, c, y, x_lo, 0], x_up)),
            lambda: (kv.at[0, c, y, x_hi, 1], x_down),
            lambda: (kv.at[0, c, y], y_up),
            lambda: (kv.at[0, c, y], y_down),
            (lambda: (kv.at[0, c, y], y_far)) if P2_DIRECT
            else (lambda: (kv.at[0, c, y_lo, pl.ds(0, 2)], y_up)),
            lambda: (kv.at[0, c, y_hi, pl.ds(2, 2)], y_down),
            lambda: (kv.at[1, c, y, x], y_up),
            lambda: (kv.at[1, c, y, x], y_down),
            (lambda: (kv.at[1, c, y, x], y_far)) if P1_DIRECT
            else (lambda: (kv.at[1, c, y_lo, x, 0], y_up)),
            lambda: (kv.at[1, c, y_hi, x, 1], y_down),
            lambda: (kv.at[1, c, :, x], x_up),
            lambda: (kv.at[1, c, :, x], x_down),
            (lambda: (kv.at[1, c, :, x], x_far)) if P2_DIRECT
            else (lambda: (kv.at[1, c, pl.ds(0, 2), x_lo], x_up)),
            lambda: (kv.at[1, c, pl.ds(2, 2), x_hi], x_down),
        ]
        if number < 25:
            place, target = places[number]()
            source = place
        else:
            rest = pl.ds(pl.multiple_of((c - NC // 2) * R, R), R)
            source, place, target = q_away.at[:, rest], q_here.at[0, :, rest], partner
        return pltpu.make_async_remote_copy(
            src_ref=source, dst_ref=place, send_sem=c_send.at[c, number], recv_sem=c_recv.at[c, number],
            device_id=target, device_id_type=MESH,
        )

    def start(numbers, c):
        for number in numbers:
            copy_c(number, c).start()

    def arrive(numbers, c):
        for number in numbers:
            copy_c(number, c).wait_recv()

    def rotate(field, cos_rows, sin_rows):
        return field * cos_rows + pltpu.roll(field, HEAD_DIM // 2, 1) * sin_rows

    def project(c):
        rows = pl.ds(pl.multiple_of(c * R, R), R)
        squares = jnp.zeros((R, 512), jnp.float32)
        for piece in range(8):
            values = gathered[piece, rows].astype(jnp.float32)
            squares = squares + values * values
        scale = lax.rsqrt(jnp.sum(squares, axis=1, keepdims=True) * (1.0 / WIDTH) + 1e-05)
        total = jnp.zeros((R, 768), jnp.float32)
        for piece in range(8):
            values = gathered[piece, rows].astype(jnp.float32)
            normed = (values * scale * gain[piece * 512:(piece + 1) * 512].astype(jnp.float32).reshape(1, 512)).astype(jnp.bfloat16)
            total = total + jnp.dot(
                normed, wqkv[piece * 512:(piece + 1) * 512, :], preferred_element_type=jnp.float32
            )
        cos_rows, sin_rows = cosine[rows], sine[rows]
        kv[0, c, y, x, z_lo] = rotate(total[:, 512:640], cos_rows, sin_rows).astype(jnp.bfloat16)
        kv[1, c, y, x, z_lo] = total[:, 640:768].astype(jnp.bfloat16)
        queries = [
            rotate(total[:, h * 128:(h + 1) * 128], cos_rows, sin_rows).astype(jnp.bfloat16) for h in range(4)
        ]

        @pl.when(c < NC // 2)
        def _():
            for h in range(4):
                q_here[1, h, rows] = queries[h]

        @pl.when(c >= NC // 2)
        def _():
            rest = pl.ds(pl.multiple_of((c - NC // 2) * R, R), R)
            for h in range(4):
                q_away[h, rest] = queries[h]

    top[...] = jnp.full(top.shape, -1e30, jnp.float32)
    denom[...] = jnp.zeros(denom.shape, jnp.float32)
    acc[...] = jnp.zeros(acc.shape, jnp.float32)
    factor_log = LOG2E / HEAD_DIM ** 0.5

    def fold(c, half, group, masked):
        keys = kv[0, c, group].reshape(CHUNK_KEYS, HEAD_DIM)
        values = kv[1, c, group].reshape(CHUNK_KEYS, HEAD_DIM)
        queries = q_here[half].reshape(4 * HALF, HEAD_DIM)
        scores = lax.dot_general(
            queries, keys, (((1,), (1,)), ((), ())), preferred_element_type=jnp.float32
        )
        if masked:
            row = lax.broadcasted_iota(jnp.int32, (4 * HALF, 1), 0) % HALF + (1 - half) * HALF
            column = lax.broadcasted_iota(jnp.int32, (1, CHUNK_KEYS), 1)
            block = (column // R) % 2 * 4 + column // (2 * R)
            key_row = (block - (z_lo * 4 + x)) * ROWS + c * R + column % R
            scores = jnp.where(key_row <= row, scores, -2e30)
        old = top[half]
        newest = jnp.maximum(old, jnp.max(scores, axis=1, keepdims=True))
        top[half] = newest
        shrink = jnp.exp2((old - newest) * factor_log)
        wide = jnp.concatenate([newest] * (CHUNK_KEYS // 128), axis=1)
        weights = jnp.exp2((scores - wide) * factor_log)
        part = weights[:, 0:128]
        for at in range(1, CHUNK_KEYS // 128):
            part = part + weights[:, at * 128:(at + 1) * 128]
        denom[half] = denom[half] * shrink + part
        acc[half] = acc[half] * shrink + jnp.dot(
            weights.astype(jnp.bfloat16), values, preferred_element_type=jnp.float32
        )

    def attend(c):
        groups_away = 3 - y

        def body(step, carry):
            half = (step >= groups_away).astype(jnp.int32)
            group = step - half * groups_away
            fold(c, half, group, False)
            return carry

        lax.fori_loop(0, 3, body, 0)

        def diagonal(half, carry):
            fold(c, half, jnp.where(half == 0, 3 - y, y), True)
            return carry

        lax.fori_loop(0, 2, diagonal, 0)

    own = (0, 1, 3, 2) if A_DIRECT else (0, 1, 2)
    if P2_DIRECT:
        spread, last = (13, 14, 15, 21, 22, 23), (13, 14, 15, 21, 22, 23)
    else:
        spread, last = (13, 14, 21, 22), (15, 16, 23, 24)
    if P1_DIRECT:
        near = (9, 10, 11, 17, 18, 19)
    else:
        near = (9, 10, 17, 18)

    for c in range(AHEAD):
        start(own, c)

    def during(t, lag):
        return (t >= lag) & (t < NC + lag)

    def tick(t, carry):
        if not P2_DIRECT:
            @pl.when(during(t, LAG_S4))
            def _():
                arrive((13, 14), t - LAG_S4)
                start((15, 16), t - LAG_S4)
                arrive((21, 22), t - LAG_S4)
                start((23, 24), t - LAG_S4)

        @pl.when(during(t, LAG_S3))
        def _():
            arrive(near if P1_DIRECT else (11, 12, 19, 20), t - LAG_S3)
            start(spread, t - LAG_S3)

        if not P1_DIRECT:
            @pl.when(during(t, LAG_S2))
            def _():
                arrive((9, 10), t - LAG_S2)
                start((11, 12), t - LAG_S2)
                arrive((17, 18), t - LAG_S2)
                start((19, 20), t - LAG_S2)

        @pl.when(during(t, LAG_S1))
        def _():
            arrive((8,), t - LAG_S1)
            start(near, t - LAG_S1)

        if not A_DIRECT:
            @pl.when(during(t, LAG_A3))
            def _():
                arrive((3, 4), t - LAG_A3)
                start((7,), t - LAG_A3)

        @pl.when(t < NC)
        def _():
            if A_DIRECT:
                arrive((0, 1, 3), t)
                start((5, 6, 7), t)
            else:
                arrive((0, 1), t)
                start((3, 4, 5, 6), t)

        @pl.when(t + AHEAD < NC)
        def _():
            start(own, t + AHEAD)

        @pl.when(t == LAG_P)
        def _():
            for copy in weights[:3]:
                copy.wait()

        @pl.when(during(t, LAG_P))
        def _():
            arrive((2, 5, 6, 7), t - LAG_P)
            project(t - LAG_P)
            start((8,), t - LAG_P)

        @pl.when((t >= NC // 2 + LAG_P) & (t < NC + LAG_P))
        def _():
            start((25,), t - LAG_P)

        @pl.when(t == LAG_ATT)
        def _():
            for c in range(NC // 2, NC):
                arrive((25,), c)

        @pl.when(t >= LAG_ATT)
        def _():
            arrive(last, t - LAG_ATT)
            attend(t - LAG_ATT)

        return carry

    lax.fori_loop(0, NC + LAG_ATT, tick, 0)

    for half in range(2):
        whole = acc[half] / jnp.sum(denom[half], axis=1, keepdims=True)
        for h in range(4):
            att[half * HALF:(half + 1) * HALF, h * 128:(h + 1) * 128] = whole[
                h * HALF:(h + 1) * HALF
            ].astype(jnp.bfloat16)
    weights[3].wait()

    def copy_d(number, u):
        return pltpu.make_async_remote_copy(
            **dict(zip(("src_ref", "dst_ref", "device_id"), (
                lambda: (term_away.at[u], term_in.at[u], sibling),
                lambda: (relay_out.at[0, u], relay_in.at[0, u], z_up),
                lambda: (relay_out.at[1, u], relay_in.at[1, u], z_down),
                lambda: (fin_out.at[0, u], fin_in.at[0, u], z_up),
                lambda: (fin_out.at[1, u], fin_in.at[1, u], z_down),
                lambda: (
                    back.at[pl.ds(pl.multiple_of(u * CR, CR), CR)],
                    out.at[pl.ds(pl.multiple_of(HALF + u * CR, CR), CR)],
                    partner,
                ),
            )[number]())),
            send_sem=d_send.at[u, number], recv_sem=d_recv.at[u, number], device_id_type=MESH,
        )

    def term(u, column):
        return jnp.dot(
            att[pl.ds(pl.multiple_of(u * CR, CR), CR)],
            wov[:, pl.ds(pl.multiple_of(column * 512, 512), 512)],
            preferred_element_type=jnp.float32,
        ).astype(jnp.bfloat16)

    def paired(u, at, rows):
        return term_own[u, at, rows].astype(jnp.float32) + term_in[u, at, rows].astype(jnp.float32)

    low, high = pl.ds(0, CR // 2), pl.ds(CR // 2, CR // 2)
    opposite, above, below = (z_hi + 2) % 4, (z_hi + 1) % 4, (z_hi + 3) % 4

    def out_tick(u, carry):
        @pl.when(u < ND)
        def _():
            for at in range(4):
                term_away[u, at] = term(u, at * 2 + 1 - core)
            copy_d(0, u).start()
            for at in range(4):
                term_own[u, at] = term(u, at * 2 + core)
            copy_d(0, u).wait_recv()
            relay_out[0, u] = paired(u, opposite, low).astype(jnp.bfloat16)
            copy_d(1, u).start()
            relay_out[1, u] = paired(u, opposite, high).astype(jnp.bfloat16)
            copy_d(2, u).start()

        @pl.when((u >= LAG_D3) & (u < ND + LAG_D3))
        def _():
            v = u - LAG_D3
            copy_d(1, v).wait_recv()
            fin_out[0, v, low] = (paired(v, above, low) + relay_in[0, v].astype(jnp.float32)).astype(jnp.bfloat16)
            fin_out[0, v, high] = paired(v, above, high).astype(jnp.bfloat16)
            copy_d(3, v).start()
            copy_d(2, v).wait_recv()
            fin_out[1, v, low] = paired(v, below, low).astype(jnp.bfloat16)
            fin_out[1, v, high] = (paired(v, below, high) + relay_in[1, v].astype(jnp.float32)).astype(jnp.bfloat16)
            copy_d(4, v).start()

        @pl.when(u >= LAG_D4)
        def _():
            v = u - LAG_D4
            copy_d(3, v).wait_recv()
            copy_d(4, v).wait_recv()
            whole = (
                paired(v, z_hi, pl.ds(0, CR)) + fin_in[0, v].astype(jnp.float32) + fin_in[1, v].astype(jnp.float32)
            ).astype(jnp.bfloat16)

            @pl.when(v < ND // 2)
            def _():
                back[pl.ds(pl.multiple_of(v * CR, CR), CR)] = whole
                copy_d(5, v).start()

            @pl.when(v >= ND // 2)
            def _():
                out[pl.ds(pl.multiple_of(v * CR - HALF, CR), CR)] = whole

        return carry

    lax.fori_loop(0, ND + LAG_D4, out_tick, 0)

    unused = ((4,) if A_DIRECT else ()) + ((12, 20) if P1_DIRECT else ()) + ((16, 24) if P2_DIRECT else ())

    def drain_c(c, carry):
        for number in range(25):
            if number not in unused:
                copy_c(number, c).wait_send()
        return carry

    def drain_q(c, carry):
        copy_c(25, c).wait_send()
        return carry

    def drain_d(u, carry):
        for number in range(5):
            copy_d(number, u).wait_send()
        return carry

    def drain_y(u, carry):
        copy_d(5, u).wait()
        return carry

    lax.fori_loop(0, NC, drain_c, 0)
    lax.fori_loop(NC // 2, NC, drain_q, 0)
    lax.fori_loop(0, ND, drain_d, 0)
    lax.fori_loop(0, ND // 2, drain_y, 0)


def body(tokens, norm_gain, w_query, w_key, w_value, w_output):
    half = HEAD_DIM // 2
    frequency = 500000.0 ** (-2.0 * jnp.arange(half, dtype=jnp.float32) / HEAD_DIM)
    positions = lax.axis_index("ctx") * ROWS + jnp.arange(ROWS, dtype=jnp.int32)
    angles = positions.astype(jnp.float32)[:, None] * frequency[None, :]
    cosine = jnp.cos(angles)
    sine = jnp.sin(angles)
    cosine = jnp.concatenate([cosine, cosine], axis=1)
    sine = jnp.concatenate([-sine, sine], axis=1)
    vmem = pl.BlockSpec(memory_space=pltpu.VMEM)
    hbm = pl.BlockSpec(memory_space=pl.ANY)
    bf16, f32 = jnp.bfloat16, jnp.float32
    return pl.pallas_call(
        sublayer,
        out_shape=jax.ShapeDtypeStruct((ROWS, 512), bf16),
        in_specs=[hbm] + [vmem] * 3 + [hbm] * 4,
        out_specs=vmem,
        scratch_shapes=[
            pltpu.VMEM((8, ROWS, 512), bf16),
            pltpu.VMEM((WIDTH, 768), bf16),
            pltpu.VMEM((512, WIDTH), bf16),
            pltpu.VMEM((2, NC, 4, 4, 2, R, HEAD_DIM), bf16),
            pltpu.VMEM((2, 4, HALF, HEAD_DIM), bf16),
            pltpu.VMEM((4, HALF, HEAD_DIM), bf16),
            pltpu.VMEM((2, 4 * HALF, 128), f32),
            pltpu.VMEM((2, 4 * HALF, 128), f32),
            pltpu.VMEM((2, 4 * HALF, HEAD_DIM), f32),
            pltpu.VMEM((ROWS, 512), bf16),
            pltpu.VMEM((ND, 4, CR, 512), bf16),
            pltpu.VMEM((ND, 4, CR, 512), bf16),
            pltpu.VMEM((ND, 4, CR, 512), bf16),
            pltpu.VMEM((2, ND, CR // 2, 512), bf16),
            pltpu.VMEM((2, ND, CR // 2, 512), bf16),
            pltpu.VMEM((2, ND, CR, 512), bf16),
            pltpu.VMEM((2, ND, CR, 512), bf16),
            pltpu.VMEM((HALF, 512), bf16),
            pltpu.SemaphoreType.DMA((5,)),
            pltpu.SemaphoreType.DMA((NC, NS)),
            pltpu.SemaphoreType.DMA((NC, NS)),
            pltpu.SemaphoreType.DMA((ND, MS)),
            pltpu.SemaphoreType.DMA((ND, MS)),
        ],
        compiler_params=pltpu.CompilerParams(
            collective_id=0, has_side_effects=True, vmem_limit_bytes=62 << 20
        ),
        cost_estimate=pl.CostEstimate(flops=6_000_000_000, bytes_accessed=12_000_000, transcendentals=6_000_000),
    )(tokens, norm_gain, cosine, sine, w_query, w_key, w_value, w_output)


def solution(mesh):
    placed = (P("ctx", "tp"), P(), P(None, "tp"), P(None, "tp"), P(None, "tp"), P("tp", None))
    return jax.shard_map(
        body, mesh=mesh, in_specs=placed, out_specs=P("ctx", "tp"), check_vma=False
    )
```

```python
import functools

import jax
import jax.numpy as jnp
from jax import lax
from jax.experimental import pallas as pl
from jax.experimental.pallas import tpu as pltpu
from jax.sharding import PartitionSpec as P

HEAD_DIM = 128
MESH = pl.DeviceIdType.MESH
ROWS = 256
HALF = 128
WIDTH = 4096
NC = 4
R = ROWS // NC
NS = 24
ND = 4
CR = ROWS // ND
MS = 6
AHEAD = 4
LAG_S3, LAG_ATT = 2, 5
LAG_D3, LAG_D4 = 1, 3
CHUNK_KEYS = 4 * R
LOG2E = 1.4426950408889634


def device_at(x, y, z_hi, z_lo, core):
    return ((y % 4) * 8 + z_lo * 4 + x % 4, (z_hi % 4) * 2 + core)


def sublayer(
    tok, gain, cosine, sine, wq, wk, wv, wo, out,
    gathered, wqkv, wov, kv, q_here, q_away, top, denom, acc, att,
    term_away, term_in, term_own, relay_out, relay_in, fin_out, fin_in, back,
    part_out, part_in, log_out, log_in,
    w_sem, c_send, c_recv, d_send, d_recv, o_send, o_recv,
):
    ctx = lax.axis_index("ctx")
    tp = lax.axis_index("tp")
    x, y, z_lo = ctx % 4, ctx // 8, (ctx // 4) % 2
    z_hi, core = tp // 2, tp % 2
    z_up = device_at(x, y, z_hi + 1, z_lo, core)
    z_down = device_at(x, y, z_hi + 3, z_lo, core)
    sibling = device_at(x, y, z_hi, z_lo, 1 - core)
    z_pair = device_at(x, y, z_hi, 1 - z_lo, core)
    x_up = device_at(x + 1, y, z_hi, z_lo, core)
    x_down = device_at(x + 3, y, z_hi, z_lo, core)
    y_up = device_at(x, y + 1, z_hi, z_lo, core)
    y_down = device_at(x, y + 3, z_hi, z_lo, core)
    partner = device_at(x, 3 - y, z_hi, z_lo, core)
    diagonal_peer = device_at(x, 3 - y, z_hi, 1 - z_lo, core)
    x_far = device_at(x + 2, y, z_hi, z_lo, core)
    y_far = device_at(x, y + 2, z_hi, z_lo, core)
    z_far = device_at(x, y, z_hi + 2, z_lo, core)

    weights = [
        pltpu.make_async_copy(wq, wqkv.at[:, pl.ds(0, 512)], w_sem.at[0]),
        pltpu.make_async_copy(wk, wqkv.at[:, pl.ds(512, 128)], w_sem.at[1]),
        pltpu.make_async_copy(wv, wqkv.at[:, pl.ds(640, 128)], w_sem.at[2]),
        pltpu.make_async_copy(wo, wov, w_sem.at[3]),
    ]
    own_tokens = pltpu.make_async_copy(tok, gathered.at[tp], w_sem.at[4])
    own_tokens.start()
    for copy in weights:
        copy.start()

    barrier = pltpu.get_barrier_semaphore()
    peers = (z_up, z_down, z_far, sibling, z_pair, diagonal_peer, x_up, x_down, x_far, y_up, y_down, y_far)
    for peer in peers:
        pl.semaphore_signal(barrier, inc=1, device_id=peer, device_id_type=MESH)
    own_tokens.wait()
    pl.semaphore_wait(barrier, len(peers))

    def copy_c(number, c):
        rows = pl.ds(pl.multiple_of(c * R, R), R)
        tokens = [gathered.at[(tp + back_by) % 8, rows] for back_by in (0, 6, 2, 4)]
        places = [
            (tokens[0], z_up), (tokens[0], z_down), (tokens[0], z_far), (tokens[0], sibling),
            (tokens[1], sibling), (tokens[2], sibling), (tokens[3], sibling),
        ]
        for other in (x_up, x_down, x_far):
            places.append((kv.at[0, c, y, x], other))
        for other in (y_up, y_down, y_far):
            places.append((kv.at[1, c, y, x], other))
        for other in (y_up, y_down, y_far):
            places.append((kv.at[0, c, y], other))
        for other in (x_up, x_down, x_far):
            places.append((kv.at[1, c, :, x], other))
        if number < 19:
            place, target = places[number]
            source = place
        elif number == 19:
            source, place, target = q_here.at[z_lo, 1, :, rows], q_here.at[z_lo, 1, :, rows], z_pair
        else:
            rest = pl.ds(pl.multiple_of((c - NC // 2) * R, R), R)
            source, place = q_away.at[:, rest], q_here.at[z_lo, 0, :, rest]
            target = partner if number == 20 else diagonal_peer
        return pltpu.make_async_remote_copy(
            src_ref=source, dst_ref=place, send_sem=c_send.at[c, number], recv_sem=c_recv.at[c, number],
            device_id=target, device_id_type=MESH,
        )

    def start(numbers, c):
        for number in numbers:
            copy_c(number, c).start()

    def arrive(numbers, c):
        for number in numbers:
            copy_c(number, c).wait_recv()

    def rotate(field, cos_rows, sin_rows):
        return field * cos_rows + pltpu.roll(field, HEAD_DIM // 2, 1) * sin_rows

    def project(c):
        rows = pl.ds(pl.multiple_of(c * R, R), R)
        squares = jnp.zeros((R, 512), jnp.float32)
        for piece in range(8):
            values = gathered[piece, rows].astype(jnp.float32)
            squares = squares + values * values
        scale = lax.rsqrt(jnp.sum(squares, axis=1, keepdims=True) * (1.0 / WIDTH) + 1e-05)
        total = jnp.zeros((R, 768), jnp.float32)
        for piece in range(8):
            values = gathered[piece, rows].astype(jnp.float32)
            normed = (values * scale * gain[piece * 512:(piece + 1) * 512].astype(jnp.float32).reshape(1, 512)).astype(jnp.bfloat16)
            total = total + jnp.dot(
                normed, wqkv[piece * 512:(piece + 1) * 512, :], preferred_element_type=jnp.float32
            )
        cos_rows, sin_rows = cosine[rows], sine[rows]
        kv[0, c, y, x] = rotate(total[:, 512:640], cos_rows, sin_rows).astype(jnp.bfloat16)
        kv[1, c, y, x] = total[:, 640:768].astype(jnp.bfloat16)
        queries = [
            rotate(total[:, h * 128:(h + 1) * 128], cos_rows, sin_rows).astype(jnp.bfloat16) for h in range(4)
        ]

        @pl.when(c < NC // 2)
        def _():
            for h in range(4):
                q_here[z_lo, 1, h, rows] = queries[h]

        @pl.when(c >= NC // 2)
        def _():
            rest = pl.ds(pl.multiple_of((c - NC // 2) * R, R), R)
            for h in range(4):
                q_away[h, rest] = queries[h]

    top[...] = jnp.full(top.shape, -1e30, jnp.float32)
    denom[...] = jnp.zeros(denom.shape, jnp.float32)
    acc[...] = jnp.zeros(acc.shape, jnp.float32)
    factor_log = LOG2E / HEAD_DIM ** 0.5

    def fold(c, half, group, masked):
        keys = kv[0, c, group].reshape(CHUNK_KEYS, HEAD_DIM)
        values = kv[1, c, group].reshape(CHUNK_KEYS, HEAD_DIM)
        queries = q_here[:, half].reshape(8 * HALF, HEAD_DIM)
        scores = lax.dot_general(
            queries, keys, (((1,), (1,)), ((), ())), preferred_element_type=jnp.float32
        )
        if masked:
            index = lax.broadcasted_iota(jnp.int32, (8 * HALF, 1), 0)
            row = (index // (4 * HALF) * 4 + x) * ROWS + index % HALF + (1 - half) * HALF
            column = lax.broadcasted_iota(jnp.int32, (1, CHUNK_KEYS), 1)
            key_row = (z_lo * 4 + column // R) * ROWS + c * R + column % R
            scores = jnp.where(key_row <= row, scores, -2e30)
        old = top[half]
        newest = jnp.maximum(old, jnp.max(scores, axis=1, keepdims=True))
        top[half] = newest
        shrink = jnp.exp2((old - newest) * factor_log)
        wide = jnp.concatenate([newest] * (CHUNK_KEYS // 128), axis=1)
        weights = jnp.exp2((scores - wide) * factor_log)
        part = weights[:, 0:128]
        for at in range(1, CHUNK_KEYS // 128):
            part = part + weights[:, at * 128:(at + 1) * 128]
        denom[half] = denom[half] * shrink + part
        acc[half] = acc[half] * shrink + jnp.dot(
            weights.astype(jnp.bfloat16), values, preferred_element_type=jnp.float32
        )

    def attend(c):
        groups_away = 3 - y

        def body(step, carry):
            half = (step >= groups_away).astype(jnp.int32)
            group = step - half * groups_away
            fold(c, half, group, False)
            return carry

        lax.fori_loop(0, 3, body, 0)

        def diagonal(half, carry):
            fold(c, half, jnp.where(half == 0, 3 - y, y), True)
            return carry

        lax.fori_loop(0, 2, diagonal, 0)

    for c in range(AHEAD):
        start((0, 1, 2, 3), c)

    def during(t, lag):
        return (t >= lag) & (t < NC + lag)

    def tick(t, carry):
        @pl.when(during(t, LAG_S3))
        def _():
            arrive(range(7, 13), t - LAG_S3)
            start(range(13, 19), t - LAG_S3)

        @pl.when(t < NC)
        def _():
            arrive((0, 1, 2), t)
            start((4, 5, 6), t)

        @pl.when(t == 1)
        def _():
            for copy in weights[:3]:
                copy.wait()

        @pl.when(during(t, 1))
        def _():
            arrive((3, 4, 5, 6), t - 1)
            project(t - 1)
            start(range(7, 13), t - 1)

        @pl.when((t >= 1) & (t < NC // 2 + 1))
        def _():
            start((19,), t - 1)

        @pl.when((t >= NC // 2 + 1) & (t < NC + 1))
        def _():
            start((20, 21), t - 1)

        @pl.when(t == LAG_ATT)
        def _():
            for c in range(NC // 2):
                arrive((19,), c)
            for c in range(NC // 2, NC):
                arrive((20, 21), c)

        @pl.when(t >= LAG_ATT)
        def _():
            arrive(range(13, 19), t - LAG_ATT)
            attend(t - LAG_ATT)

        return carry

    lax.fori_loop(0, NC + LAG_ATT, tick, 0)

    def returned(at):
        source, place = ((part_out.at[at], part_in.at[at]) if at < 2 else (log_out, log_in))
        return pltpu.make_async_remote_copy(
            src_ref=source, dst_ref=place, send_sem=o_send.at[at], recv_sem=o_recv.at[at],
            device_id=z_pair, device_id_type=MESH,
        )

    def partial(half, side):
        rows = pl.ds(pl.multiple_of(side * 4 * HALF, 4 * HALF), 4 * HALF)
        return acc[half, rows], top[half, rows], jnp.sum(denom[half, rows], axis=1, keepdims=True)

    for half in range(2):
        whole, highest, total = partial(half, 1 - z_lo)
        part_out[half] = (whole / jnp.where(total > 0.0, total, 1.0)).astype(jnp.bfloat16)
        returned(half).start()
        log_out[half, 0] = highest.T[0:8]
        log_out[half, 1] = jnp.broadcast_to(total, (4 * HALF, 128)).T[0:8]
    returned(2).start()
    for at in range(3):
        returned(at).wait()
    for half in range(2):
        whole, highest, total = partial(half, z_lo)
        other_highest = jnp.broadcast_to(log_in[half, 0, 0:1], (128, 4 * HALF)).T
        other_total = jnp.broadcast_to(log_in[half, 1, 0:1], (128, 4 * HALF)).T
        common = jnp.maximum(highest, other_highest)
        mine = jnp.exp2((highest - common) * factor_log)
        theirs = jnp.exp2((other_highest - common) * factor_log) * other_total
        whole = (whole * mine + part_in[half].astype(jnp.float32) * theirs) / (total * mine + theirs)
        for h in range(4):
            att[half * HALF:(half + 1) * HALF, h * 128:(h + 1) * 128] = whole[
                h * HALF:(h + 1) * HALF
            ].astype(jnp.bfloat16)
    weights[3].wait()

    def copy_d(number, u):
        return pltpu.make_async_remote_copy(
            **dict(zip(("src_ref", "dst_ref", "device_id"), (
                lambda: (term_away.at[u], term_in.at[u], sibling),
                lambda: (relay_out.at[0, u], relay_in.at[0, u], z_up),
                lambda: (relay_out.at[1, u], relay_in.at[1, u], z_down),
                lambda: (fin_out.at[0, u], fin_in.at[0, u], z_up),
                lambda: (fin_out.at[1, u], fin_in.at[1, u], z_down),
                lambda: (
                    back.at[pl.ds(pl.multiple_of(u * CR, CR), CR)],
                    out.at[pl.ds(pl.multiple_of(HALF + u * CR, CR), CR)],
                    partner,
                ),
            )[number]())),
            send_sem=d_send.at[u, number], recv_sem=d_recv.at[u, number], device_id_type=MESH,
        )

    def term(u, column):
        return jnp.dot(
            att[pl.ds(pl.multiple_of(u * CR, CR), CR)],
            wov[:, pl.ds(pl.multiple_of(column * 512, 512), 512)],
            preferred_element_type=jnp.float32,
        ).astype(jnp.bfloat16)

    def paired(u, at, rows):
        return term_own[u, at, rows].astype(jnp.float32) + term_in[u, at, rows].astype(jnp.float32)

    low, high = pl.ds(0, CR // 2), pl.ds(CR // 2, CR // 2)
    opposite, above, below = (z_hi + 2) % 4, (z_hi + 1) % 4, (z_hi + 3) % 4

    def out_tick(u, carry):
        @pl.when(u < ND)
        def _():
            for at in range(4):
                term_away[u, at] = term(u, at * 2 + 1 - core)
            copy_d(0, u).start()
            for at in range(4):
                term_own[u, at] = term(u, at * 2 + core)
            copy_d(0, u).wait_recv()
            relay_out[0, u] = paired(u, opposite, low).astype(jnp.bfloat16)
            copy_d(1, u).start()
            relay_out[1, u] = paired(u, opposite, high).astype(jnp.bfloat16)
            copy_d(2, u).start()

        @pl.when((u >= LAG_D3) & (u < ND + LAG_D3))
        def _():
            v = u - LAG_D3
            copy_d(1, v).wait_recv()
            fin_out[0, v, low] = (paired(v, above, low) + relay_in[0, v].astype(jnp.float32)).astype(jnp.bfloat16)
            fin_out[0, v, high] = paired(v, above, high).astype(jnp.bfloat16)
            copy_d(3, v).start()
            copy_d(2, v).wait_recv()
            fin_out[1, v, low] = paired(v, below, low).astype(jnp.bfloat16)
            fin_out[1, v, high] = (paired(v, below, high) + relay_in[1, v].astype(jnp.float32)).astype(jnp.bfloat16)
            copy_d(4, v).start()

        @pl.when(u >= LAG_D4)
        def _():
            v = u - LAG_D4
            copy_d(3, v).wait_recv()
            copy_d(4, v).wait_recv()
            whole = (
                paired(v, z_hi, pl.ds(0, CR)) + fin_in[0, v].astype(jnp.float32) + fin_in[1, v].astype(jnp.float32)
            ).astype(jnp.bfloat16)

            @pl.when(v < ND // 2)
            def _():
                back[pl.ds(pl.multiple_of(v * CR, CR), CR)] = whole
                copy_d(5, v).start()

            @pl.when(v >= ND // 2)
            def _():
                out[pl.ds(pl.multiple_of(v * CR - HALF, CR), CR)] = whole

        return carry

    lax.fori_loop(0, ND + LAG_D4, out_tick, 0)

    def drain_c(c, carry):
        for number in range(19):
            copy_c(number, c).wait_send()
        return carry

    def drain_near(c, carry):
        copy_c(19, c).wait_send()
        return carry

    def drain_q(c, carry):
        copy_c(20, c).wait_send()
        copy_c(21, c).wait_send()
        return carry

    def drain_d(u, carry):
        for number in range(5):
            copy_d(number, u).wait_send()
        return carry

    def drain_y(u, carry):
        copy_d(5, u).wait()
        return carry

    lax.fori_loop(0, NC, drain_c, 0)
    lax.fori_loop(0, NC // 2, drain_near, 0)
    lax.fori_loop(NC // 2, NC, drain_q, 0)
    lax.fori_loop(0, ND, drain_d, 0)
    lax.fori_loop(0, ND // 2, drain_y, 0)


def body(tokens, norm_gain, w_query, w_key, w_value, w_output):
    half = HEAD_DIM // 2
    frequency = 500000.0 ** (-2.0 * jnp.arange(half, dtype=jnp.float32) / HEAD_DIM)
    positions = lax.axis_index("ctx") * ROWS + jnp.arange(ROWS, dtype=jnp.int32)
    angles = positions.astype(jnp.float32)[:, None] * frequency[None, :]
    cosine = jnp.cos(angles)
    sine = jnp.sin(angles)
    cosine = jnp.concatenate([cosine, cosine], axis=1)
    sine = jnp.concatenate([-sine, sine], axis=1)
    vmem = pl.BlockSpec(memory_space=pltpu.VMEM)
    hbm = pl.BlockSpec(memory_space=pl.ANY)
    bf16, f32 = jnp.bfloat16, jnp.float32
    return pl.pallas_call(
        sublayer,
        out_shape=jax.ShapeDtypeStruct((ROWS, 512), bf16),
        in_specs=[hbm] + [vmem] * 3 + [hbm] * 4,
        out_specs=vmem,
        scratch_shapes=[
            pltpu.VMEM((8, ROWS, 512), bf16),
            pltpu.VMEM((WIDTH, 768), bf16),
            pltpu.VMEM((512, WIDTH), bf16),
            pltpu.VMEM((2, NC, 4, 4, R, HEAD_DIM), bf16),
            pltpu.VMEM((2, 2, 4, HALF, HEAD_DIM), bf16),
            pltpu.VMEM((4, HALF, HEAD_DIM), bf16),
            pltpu.VMEM((2, 8 * HALF, 128), f32),
            pltpu.VMEM((2, 8 * HALF, 128), f32),
            pltpu.VMEM((2, 8 * HALF, HEAD_DIM), f32),
            pltpu.VMEM((ROWS, 512), bf16),
            pltpu.VMEM((ND, 4, CR, 512), bf16),
            pltpu.VMEM((ND, 4, CR, 512), bf16),
            pltpu.VMEM((ND, 4, CR, 512), bf16),
            pltpu.VMEM((2, ND, CR // 2, 512), bf16),
            pltpu.VMEM((2, ND, CR // 2, 512), bf16),
            pltpu.VMEM((2, ND, CR, 512), bf16),
            pltpu.VMEM((2, ND, CR, 512), bf16),
            pltpu.VMEM((HALF, 512), bf16),
            pltpu.VMEM((2, 4 * HALF, HEAD_DIM), bf16),
            pltpu.VMEM((2, 4 * HALF, HEAD_DIM), bf16),
            pltpu.VMEM((2, 2, 8, 4 * HALF), f32),
            pltpu.VMEM((2, 2, 8, 4 * HALF), f32),
            pltpu.SemaphoreType.DMA((5,)),
            pltpu.SemaphoreType.DMA((NC, NS)),
            pltpu.SemaphoreType.DMA((NC, NS)),
            pltpu.SemaphoreType.DMA((ND, MS)),
            pltpu.SemaphoreType.DMA((ND, MS)),
            pltpu.SemaphoreType.DMA((3,)),
            pltpu.SemaphoreType.DMA((3,)),
        ],
        compiler_params=pltpu.CompilerParams(
            collective_id=0, has_side_effects=True, vmem_limit_bytes=62 << 20
        ),
        cost_estimate=pl.CostEstimate(flops=6_000_000_000, bytes_accessed=12_000_000, transcendentals=6_000_000),
    )(tokens, norm_gain, cosine, sine, w_query, w_key, w_value, w_output)


def solution(mesh):
    placed = (P("ctx", "tp"), P(), P(None, "tp"), P(None, "tp"), P(None, "tp"), P("tp", None))
    return jax.shard_map(
        body, mesh=mesh, in_specs=placed, out_specs=P("ctx", "tp"), check_vma=False
    )
```

```python
import functools

import jax
import jax.numpy as jnp
from jax import lax
from jax.experimental import pallas as pl
from jax.experimental.pallas import tpu as pltpu
from jax.sharding import PartitionSpec as P

HEAD_DIM = 128
MESH = pl.DeviceIdType.MESH
ROWS = 256
HALF = 128
WIDTH = 4096
NC = 4
R = ROWS // NC
NS = 26
ND = 4
CR = ROWS // ND
MS = 6
AHEAD = 3
A_DIRECT, P1_DIRECT, P2_DIRECT = False, True, False
LAG_A3, LAG_P, LAG_S1, LAG_S2, LAG_S3, LAG_S4, LAG_ATT = 2, 3, 5, 6, 7, 9, 11
LAG_D3, LAG_D4 = 1, 3
CHUNK_KEYS = 8 * R
LOG2E = 1.4426950408889634


def device_at(x, y, z_hi, z_lo, core):
    return ((y % 4) * 8 + z_lo * 4 + x % 4, (z_hi % 4) * 2 + core)


def sublayer(
    tok, gain, cosine, sine, wq, wk, wv, wo, out,
    gathered, wqkv, wov, kv, q_here, q_away, top, denom, acc, att,
    term_away, term_in, term_own, relay_out, relay_in, fin_out, fin_in, back,
    w_sem, c_send, c_recv, d_send, d_recv,
):
    ctx = lax.axis_index("ctx")
    tp = lax.axis_index("tp")
    x, y, z_lo = ctx % 4, ctx // 8, (ctx // 4) % 2
    z_hi, core = tp // 2, tp % 2
    z_up = device_at(x, y, z_hi + 1, z_lo, core)
    z_down = device_at(x, y, z_hi + 3, z_lo, core)
    sibling = device_at(x, y, z_hi, z_lo, 1 - core)
    z_pair = device_at(x, y, z_hi, 1 - z_lo, core)
    x_up = device_at(x + 1, y, z_hi, z_lo, core)
    x_down = device_at(x + 3, y, z_hi, z_lo, core)
    y_up = device_at(x, y + 1, z_hi, z_lo, core)
    y_down = device_at(x, y + 3, z_hi, z_lo, core)
    partner = device_at(x, 3 - y, z_hi, z_lo, core)
    x_far = device_at(x + 2, y, z_hi, z_lo, core)
    y_far = device_at(x, y + 2, z_hi, z_lo, core)

    weights = [
        pltpu.make_async_copy(wq, wqkv.at[:, pl.ds(0, 512)], w_sem.at[0]),
        pltpu.make_async_copy(wk, wqkv.at[:, pl.ds(512, 128)], w_sem.at[1]),
        pltpu.make_async_copy(wv, wqkv.at[:, pl.ds(640, 128)], w_sem.at[2]),
        pltpu.make_async_copy(wo, wov, w_sem.at[3]),
    ]
    own_tokens = pltpu.make_async_copy(tok, gathered.at[tp], w_sem.at[4])
    own_tokens.start()
    for copy in weights:
        copy.start()

    barrier = pltpu.get_barrier_semaphore()
    peers = (z_up, z_down, sibling, z_pair, x_up, x_down, y_up, y_down, x_far, y_far)
    for peer in peers:
        pl.semaphore_signal(barrier, inc=1, device_id=peer, device_id_type=MESH)
    own_tokens.wait()
    pl.semaphore_wait(barrier, len(peers))

    x_lo, x_hi, y_lo, y_hi = (x + 3) % 4, (x + 1) % 4, (y + 3) % 4, (y + 1) % 4

    def copy_c(number, c):
        rows = pl.ds(pl.multiple_of(c * R, R), R)
        first = pl.ds(pl.multiple_of(c * R, R // 2), R // 2)
        second = pl.ds(pl.multiple_of(c * R + R // 2, R // 2), R // 2)
        z_far = device_at(x, y, z_hi + 2, z_lo, core)
        places = [
            lambda: (gathered.at[tp, rows], z_up),
            lambda: (gathered.at[tp, rows], z_down),
            lambda: (gathered.at[tp, rows], sibling),
            (lambda: (gathered.at[tp, rows], z_far)) if A_DIRECT
            else (lambda: (gathered.at[(tp + 6) % 8, first], z_up)),
            lambda: (gathered.at[(tp + 2) % 8, second], z_down),
            lambda: (gathered.at[(tp + 6) % 8, rows], sibling),
            lambda: (gathered.at[(tp + 2) % 8, rows], sibling),
            lambda: (gathered.at[(tp + 4) % 8, rows], sibling),
            lambda: (kv.at[:, c, y, x, z_lo], z_pair),
            lambda: (kv.at[0, c, y, x], x_up),
            lambda: (kv.at[0, c, y, x], x_down),
            (lambda: (kv.at[0, c, y, x], x_far)) if P1_DIRECT
            else (lambda: (kv.at[0, c, y, x_lo, 0], x_up)),
            lambda: (kv.at[0, c, y, x_hi, 1], x_down),
            lambda: (kv.at[0, c, y], y_up),
            lambda: (kv.at[0, c, y], y_down),
            (lambda: (kv.at[0, c, y], y_far)) if P2_DIRECT
            else (lambda: (kv.at[0, c, y_lo, pl.ds(0, 2)], y_up)),
            lambda: (kv.at[0, c, y_hi, pl.ds(2, 2)], y_down),
            lambda: (kv.at[1, c, y, x], y_up),
            lambda: (kv.at[1, c, y, x], y_down),
            (lambda: (kv.at[1, c, y, x], y_far)) if P1_DIRECT
            else (lambda: (kv.at[1, c, y_lo, x, 0], y_up)),
            lambda: (kv.at[1, c, y_hi, x, 1], y_down),
            lambda: (kv.at[1, c, :, x], x_up),
            lambda: (kv.at[1, c, :, x], x_down),
            (lambda: (kv.at[1, c, :, x], x_far)) if P2_DIRECT
            else (lambda: (kv.at[1, c, pl.ds(0, 2), x_lo], x_up)),
            lambda: (kv.at[1, c, pl.ds(2, 2), x_hi], x_down),
        ]
        if number < 25:
            place, target = places[number]()
            source = place
        else:
            rest = pl.ds(pl.multiple_of((c - NC // 2) * R, R), R)
            source, place, target = q_away.at[:, rest], q_here.at[0, :, rest], partner
        return pltpu.make_async_remote_copy(
            src_ref=source, dst_ref=place, send_sem=c_send.at[c, number], recv_sem=c_recv.at[c, number],
            device_id=target, device_id_type=MESH,
        )

    def start(numbers, c):
        for number in numbers:
            copy_c(number, c).start()

    def arrive(numbers, c):
        for number in numbers:
            copy_c(number, c).wait_recv()

    def rotate(field, cos_rows, sin_rows):
        return field * cos_rows + pltpu.roll(field, HEAD_DIM // 2, 1) * sin_rows

    def project(c):
        rows = pl.ds(pl.multiple_of(c * R, R), R)
        squares = jnp.zeros((R, 512), jnp.float32)
        for piece in range(8):
            values = gathered[piece, rows].astype(jnp.float32)
            squares = squares + values * values
        scale = lax.rsqrt(jnp.sum(squares, axis=1, keepdims=True) * (1.0 / WIDTH) + 1e-05)
        total = jnp.zeros((R, 768), jnp.float32)
        for piece in range(8):
            values = gathered[piece, rows].astype(jnp.float32)
            normed = (values * scale * gain[piece * 512:(piece + 1) * 512].astype(jnp.float32).reshape(1, 512)).astype(jnp.bfloat16)
            total = total + jnp.dot(
                normed, wqkv[piece * 512:(piece + 1) * 512, :], preferred_element_type=jnp.float32
            )
        cos_rows, sin_rows = cosine[rows], sine[rows]
        kv[0, c, y, x, z_lo] = rotate(total[:, 512:640], cos_rows, sin_rows).astype(jnp.bfloat16)
        kv[1, c, y, x, z_lo] = total[:, 640:768].astype(jnp.bfloat16)
        queries = [
            rotate(total[:, h * 128:(h + 1) * 128], cos_rows, sin_rows).astype(jnp.bfloat16) for h in range(4)
        ]

        @pl.when(c < NC // 2)
        def _():
            for h in range(4):
                q_here[1, h, rows] = queries[h]

        @pl.when(c >= NC // 2)
        def _():
            rest = pl.ds(pl.multiple_of((c - NC // 2) * R, R), R)
            for h in range(4):
                q_away[h, rest] = queries[h]

    top[...] = jnp.full(top.shape, -1e30, jnp.float32)
    denom[...] = jnp.zeros(denom.shape, jnp.float32)
    acc[...] = jnp.zeros(acc.shape, jnp.float32)
    factor_log = LOG2E / HEAD_DIM ** 0.5

    def fold(c, half, group, masked):
        keys = kv[0, c, group].reshape(CHUNK_KEYS, HEAD_DIM)
        values = kv[1, c, group].reshape(CHUNK_KEYS, HEAD_DIM)
        queries = q_here[half].reshape(4 * HALF, HEAD_DIM)
        scores = lax.dot_general(
            queries, keys, (((1,), (1,)), ((), ())), preferred_element_type=jnp.float32
        )
        if masked:
            row = lax.broadcasted_iota(jnp.int32, (4 * HALF, 1), 0) % HALF + (1 - half) * HALF
            column = lax.broadcasted_iota(jnp.int32, (1, CHUNK_KEYS), 1)
            block = (column // R) % 2 * 4 + column // (2 * R)
            key_row = (block - (z_lo * 4 + x)) * ROWS + c * R + column % R
            scores = jnp.where(key_row <= row, scores, -2e30)
        old = top[half]
        newest = jnp.maximum(old, jnp.max(scores, axis=1, keepdims=True))
        top[half] = newest
        shrink = jnp.exp2((old - newest) * factor_log)
        wide = jnp.concatenate([newest] * (CHUNK_KEYS // 128), axis=1)
        weights = jnp.exp2((scores - wide) * factor_log)
        part = weights[:, 0:128]
        for at in range(1, CHUNK_KEYS // 128):
            part = part + weights[:, at * 128:(at + 1) * 128]
        denom[half] = denom[half] * shrink + part
        acc[half] = acc[half] * shrink + jnp.dot(
            weights.astype(jnp.bfloat16), values, preferred_element_type=jnp.float32
        )

    def attend(c):
        groups_away = 3 - y

        def body(step, carry):
            half = (step >= groups_away).astype(jnp.int32)
            group = step - half * groups_away
            fold(c, half, group, False)
            return carry

        lax.fori_loop(0, 3, body, 0)

        def diagonal(half, carry):
            fold(c, half, jnp.where(half == 0, 3 - y, y), True)
            return carry

        lax.fori_loop(0, 2, diagonal, 0)

    own = (0, 1, 3, 2) if A_DIRECT else (0, 1, 2)
    if P2_DIRECT:
        spread, last = (13, 14, 15, 21, 22, 23), (13, 14, 15, 21, 22, 23)
    else:
        spread, last = (13, 14, 21, 22), (15, 16, 23, 24)
    if P1_DIRECT:
        near = (9, 10, 11, 17, 18, 19)
    else:
        near = (9, 10, 17, 18)

    for c in range(AHEAD):
        start(own, c)

    def during(t, lag):
        return (t >= lag) & (t < NC + lag)

    def tick(t, carry):
        if not P2_DIRECT:
            @pl.when(during(t, LAG_S4))
            def _():
                arrive((13, 14), t - LAG_S4)
                start((15, 16), t - LAG_S4)
                arrive((21, 22), t - LAG_S4)
                start((23, 24), t - LAG_S4)

        @pl.when(during(t, LAG_S3))
        def _():
            arrive(near if P1_DIRECT else (11, 12, 19, 20), t - LAG_S3)
            start(spread, t - LAG_S3)

        if not P1_DIRECT:
            @pl.when(during(t, LAG_S2))
            def _():
                arrive((9, 10), t - LAG_S2)
                start((11, 12), t - LAG_S2)
                arrive((17, 18), t - LAG_S2)
                start((19, 20), t - LAG_S2)

        @pl.when(during(t, LAG_S1))
        def _():
            arrive((8,), t - LAG_S1)
            start(near, t - LAG_S1)

        if not A_DIRECT:
            @pl.when(during(t, LAG_A3))
            def _():
                arrive((3, 4), t - LAG_A3)
                start((7,), t - LAG_A3)

        @pl.when(t < NC)
        def _():
            if A_DIRECT:
                arrive((0, 1, 3), t)
                start((5, 6, 7), t)
            else:
                arrive((0, 1), t)
                start((3, 4, 5, 6), t)

        @pl.when(t + AHEAD < NC)
        def _():
            start(own, t + AHEAD)

        @pl.when(t == LAG_P)
        def _():
            for copy in weights[:3]:
                copy.wait()

        @pl.when(during(t, LAG_P))
        def _():
            arrive((2, 5, 6, 7), t - LAG_P)
            project(t - LAG_P)
            start((8,), t - LAG_P)

        @pl.when((t >= NC // 2 + LAG_P) & (t < NC + LAG_P))
        def _():
            start((25,), t - LAG_P)

        @pl.when(t == LAG_ATT)
        def _():
            for c in range(NC // 2, NC):
                arrive((25,), c)

        @pl.when(t >= LAG_ATT)
        def _():
            arrive(last, t - LAG_ATT)
            attend(t - LAG_ATT)

        return carry

    lax.fori_loop(0, NC + LAG_ATT, tick, 0)

    for half in range(2):
        whole = acc[half] / jnp.sum(denom[half], axis=1, keepdims=True)
        for h in range(4):
            att[half * HALF:(half + 1) * HALF, h * 128:(h + 1) * 128] = whole[
                h * HALF:(h + 1) * HALF
            ].astype(jnp.bfloat16)
    weights[3].wait()

    def copy_d(number, u):
        return pltpu.make_async_remote_copy(
            **dict(zip(("src_ref", "dst_ref", "device_id"), (
                lambda: (term_away.at[u], term_in.at[u], sibling),
                lambda: (relay_out.at[0, u], relay_in.at[0, u], z_up),
                lambda: (relay_out.at[1, u], relay_in.at[1, u], z_down),
                lambda: (fin_out.at[0, u], fin_in.at[0, u], z_up),
                lambda: (fin_out.at[1, u], fin_in.at[1, u], z_down),
                lambda: (
                    back.at[pl.ds(pl.multiple_of(u * CR, CR), CR)],
                    out.at[pl.ds(pl.multiple_of(HALF + u * CR, CR), CR)],
                    partner,
                ),
            )[number]())),
            send_sem=d_send.at[u, number], recv_sem=d_recv.at[u, number], device_id_type=MESH,
        )

    def term(u, column):
        return jnp.dot(
            att[pl.ds(pl.multiple_of(u * CR, CR), CR)],
            wov[:, pl.ds(pl.multiple_of(column * 512, 512), 512)],
            preferred_element_type=jnp.float32,
        ).astype(jnp.bfloat16)

    def paired(u, at, rows):
        return term_own[u, at, rows].astype(jnp.float32) + term_in[u, at, rows].astype(jnp.float32)

    low, high = pl.ds(0, CR // 2), pl.ds(CR // 2, CR // 2)
    opposite, above, below = (z_hi + 2) % 4, (z_hi + 1) % 4, (z_hi + 3) % 4

    def out_tick(u, carry):
        @pl.when(u < ND)
        def _():
            for at in range(4):
                term_away[u, at] = term(u, at * 2 + 1 - core)
            copy_d(0, u).start()
            for at in range(4):
                term_own[u, at] = term(u, at * 2 + core)
            copy_d(0, u).wait_recv()
            relay_out[0, u] = paired(u, opposite, low).astype(jnp.bfloat16)
            copy_d(1, u).start()
            relay_out[1, u] = paired(u, opposite, high).astype(jnp.bfloat16)
            copy_d(2, u).start()

        @pl.when((u >= LAG_D3) & (u < ND + LAG_D3))
        def _():
            v = u - LAG_D3
            copy_d(1, v).wait_recv()
            fin_out[0, v, low] = (paired(v, above, low) + relay_in[0, v].astype(jnp.float32)).astype(jnp.bfloat16)
            fin_out[0, v, high] = paired(v, above, high).astype(jnp.bfloat16)
            copy_d(3, v).start()
            copy_d(2, v).wait_recv()
            fin_out[1, v, low] = paired(v, below, low).astype(jnp.bfloat16)
            fin_out[1, v, high] = (paired(v, below, high) + relay_in[1, v].astype(jnp.float32)).astype(jnp.bfloat16)
            copy_d(4, v).start()

        @pl.when(u >= LAG_D4)
        def _():
            v = u - LAG_D4
            copy_d(3, v).wait_recv()
            copy_d(4, v).wait_recv()
            whole = (
                paired(v, z_hi, pl.ds(0, CR)) + fin_in[0, v].astype(jnp.float32) + fin_in[1, v].astype(jnp.float32)
            ).astype(jnp.bfloat16)

            @pl.when(v < ND // 2)
            def _():
                back[pl.ds(pl.multiple_of(v * CR, CR), CR)] = whole
                copy_d(5, v).start()

            @pl.when(v >= ND // 2)
            def _():
                out[pl.ds(pl.multiple_of(v * CR - HALF, CR), CR)] = whole

        return carry

    lax.fori_loop(0, ND + LAG_D4, out_tick, 0)

    unused = ((4,) if A_DIRECT else ()) + ((12, 20) if P1_DIRECT else ()) + ((16, 24) if P2_DIRECT else ())

    def drain_c(c, carry):
        for number in range(25):
            if number not in unused:
                copy_c(number, c).wait_send()
        return carry

    def drain_q(c, carry):
        copy_c(25, c).wait_send()
        return carry

    def drain_d(u, carry):
        for number in range(5):
            copy_d(number, u).wait_send()
        return carry

    def drain_y(u, carry):
        copy_d(5, u).wait()
        return carry

    lax.fori_loop(0, NC, drain_c, 0)
    lax.fori_loop(NC // 2, NC, drain_q, 0)
    lax.fori_loop(0, ND, drain_d, 0)
    lax.fori_loop(0, ND // 2, drain_y, 0)


def body(tokens, norm_gain, w_query, w_key, w_value, w_output):
    half = HEAD_DIM // 2
    frequency = 500000.0 ** (-2.0 * jnp.arange(half, dtype=jnp.float32) / HEAD_DIM)
    positions = lax.axis_index("ctx") * ROWS + jnp.arange(ROWS, dtype=jnp.int32)
    angles = positions.astype(jnp.float32)[:, None] * frequency[None, :]
    cosine = jnp.cos(angles)
    sine = jnp.sin(angles)
    cosine = jnp.concatenate([cosine, cosine], axis=1)
    sine = jnp.concatenate([-sine, sine], axis=1)
    vmem = pl.BlockSpec(memory_space=pltpu.VMEM)
    hbm = pl.BlockSpec(memory_space=pl.ANY)
    bf16, f32 = jnp.bfloat16, jnp.float32
    return pl.pallas_call(
        sublayer,
        out_shape=jax.ShapeDtypeStruct((ROWS, 512), bf16),
        in_specs=[hbm] + [vmem] * 3 + [hbm] * 4,
        out_specs=vmem,
        scratch_shapes=[
            pltpu.VMEM((8, ROWS, 512), bf16),
            pltpu.VMEM((WIDTH, 768), bf16),
            pltpu.VMEM((512, WIDTH), bf16),
            pltpu.VMEM((2, NC, 4, 4, 2, R, HEAD_DIM), bf16),
            pltpu.VMEM((2, 4, HALF, HEAD_DIM), bf16),
            pltpu.VMEM((4, HALF, HEAD_DIM), bf16),
            pltpu.VMEM((2, 4 * HALF, 128), f32),
            pltpu.VMEM((2, 4 * HALF, 128), f32),
            pltpu.VMEM((2, 4 * HALF, HEAD_DIM), f32),
            pltpu.VMEM((ROWS, 512), bf16),
            pltpu.VMEM((ND, 4, CR, 512), bf16),
            pltpu.VMEM((ND, 4, CR, 512), bf16),
            pltpu.VMEM((ND, 4, CR, 512), bf16),
            pltpu.VMEM((2, ND, CR // 2, 512), bf16),
            pltpu.VMEM((2, ND, CR // 2, 512), bf16),
            pltpu.VMEM((2, ND, CR, 512), bf16),
            pltpu.VMEM((2, ND, CR, 512), bf16),
            pltpu.VMEM((HALF, 512), bf16),
            pltpu.SemaphoreType.DMA((5,)),
            pltpu.SemaphoreType.DMA((NC, NS)),
            pltpu.SemaphoreType.DMA((NC, NS)),
            pltpu.SemaphoreType.DMA((ND, MS)),
            pltpu.SemaphoreType.DMA((ND, MS)),
        ],
        compiler_params=pltpu.CompilerParams(
            collective_id=0, has_side_effects=True, vmem_limit_bytes=62 << 20
        ),
        cost_estimate=pl.CostEstimate(flops=6_000_000_000, bytes_accessed=12_000_000, transcendentals=6_000_000),
    )(tokens, norm_gain, cosine, sine, w_query, w_key, w_value, w_output)


def solution(mesh):
    placed = (P("ctx", "tp"), P(), P(None, "tp"), P(None, "tp"), P(None, "tp"), P("tp", None))
    return jax.shard_map(
        body, mesh=mesh, in_specs=placed, out_specs=P("ctx", "tp"), check_vma=False
    )
```

```python
import functools

import jax
import jax.numpy as jnp
from jax import lax
from jax.experimental import pallas as pl
from jax.experimental.pallas import tpu as pltpu
from jax.sharding import PartitionSpec as P

HEAD_DIM = 128
MESH = pl.DeviceIdType.MESH
ROWS = 256
HALF = 128
WIDTH = 4096
NC = 4
R = ROWS // NC
NS = 26
ND = 4
CR = ROWS // ND
MS = 6
AHEAD = 3
A_DIRECT, P1_DIRECT, P2_DIRECT = False, True, False
LAG_A3, LAG_P, LAG_S1, LAG_S2, LAG_S3, LAG_S4, LAG_ATT = 2, 3, 4, 5, 6, 8, 10
LAG_D3, LAG_D4 = 1, 3
CHUNK_KEYS = 8 * R
LOG2E = 1.4426950408889634


def device_at(x, y, z_hi, z_lo, core):
    return ((y % 4) * 8 + z_lo * 4 + x % 4, (z_hi % 4) * 2 + core)


def sublayer(
    tok, gain, cosine, sine, wq, wk, wv, wo, out,
    gathered, wqkv, wov, kv, q_here, q_away, top, denom, acc, att,
    term_away, term_in, term_own, relay_out, relay_in, fin_out, fin_in, back,
    w_sem, c_send, c_recv, d_send, d_recv,
):
    ctx = lax.axis_index("ctx")
    tp = lax.axis_index("tp")
    x, y, z_lo = ctx % 4, ctx // 8, (ctx // 4) % 2
    z_hi, core = tp // 2, tp % 2
    z_up = device_at(x, y, z_hi + 1, z_lo, core)
    z_down = device_at(x, y, z_hi + 3, z_lo, core)
    sibling = device_at(x, y, z_hi, z_lo, 1 - core)
    z_pair = device_at(x, y, z_hi, 1 - z_lo, core)
    x_up = device_at(x + 1, y, z_hi, z_lo, core)
    x_down = device_at(x + 3, y, z_hi, z_lo, core)
    y_up = device_at(x, y + 1, z_hi, z_lo, core)
    y_down = device_at(x, y + 3, z_hi, z_lo, core)
    partner = device_at(x, 3 - y, z_hi, z_lo, core)
    x_far = device_at(x + 2, y, z_hi, z_lo, core)
    y_far = device_at(x, y + 2, z_hi, z_lo, core)

    weights = [
        pltpu.make_async_copy(wq, wqkv.at[:, pl.ds(0, 512)], w_sem.at[0]),
        pltpu.make_async_copy(wk, wqkv.at[:, pl.ds(512, 128)], w_sem.at[1]),
        pltpu.make_async_copy(wv, wqkv.at[:, pl.ds(640, 128)], w_sem.at[2]),
        pltpu.make_async_copy(wo, wov, w_sem.at[3]),
    ]
    own_tokens = pltpu.make_async_copy(tok, gathered.at[tp], w_sem.at[4])
    own_tokens.start()
    for copy in weights:
        copy.start()

    barrier = pltpu.get_barrier_semaphore()
    peers = (z_up, z_down, sibling, z_pair, x_up, x_down, y_up, y_down, x_far, y_far)
    for peer in peers:
        pl.semaphore_signal(barrier, inc=1, device_id=peer, device_id_type=MESH)
    own_tokens.wait()
    pl.semaphore_wait(barrier, len(peers))

    x_lo, x_hi, y_lo, y_hi = (x + 3) % 4, (x + 1) % 4, (y + 3) % 4, (y + 1) % 4

    def copy_c(number, c):
        rows = pl.ds(pl.multiple_of(c * R, R), R)
        first = pl.ds(pl.multiple_of(c * R, R // 2), R // 2)
        second = pl.ds(pl.multiple_of(c * R + R // 2, R // 2), R // 2)
        z_far = device_at(x, y, z_hi + 2, z_lo, core)
        places = [
            lambda: (gathered.at[tp, rows], z_up),
            lambda: (gathered.at[tp, rows], z_down),
            lambda: (gathered.at[tp, rows], sibling),
            (lambda: (gathered.at[tp, rows], z_far)) if A_DIRECT
            else (lambda: (gathered.at[(tp + 6) % 8, first], z_up)),
            lambda: (gathered.at[(tp + 2) % 8, second], z_down),
            lambda: (gathered.at[(tp + 6) % 8, rows], sibling),
            lambda: (gathered.at[(tp + 2) % 8, rows], sibling),
            lambda: (gathered.at[(tp + 4) % 8, rows], sibling),
            lambda: (kv.at[:, c, y, x, z_lo], z_pair),
            lambda: (kv.at[0, c, y, x], x_up),
            lambda: (kv.at[0, c, y, x], x_down),
            (lambda: (kv.at[0, c, y, x], x_far)) if P1_DIRECT
            else (lambda: (kv.at[0, c, y, x_lo, 0], x_up)),
            lambda: (kv.at[0, c, y, x_hi, 1], x_down),
            lambda: (kv.at[0, c, y], y_up),
            lambda: (kv.at[0, c, y], y_down),
            (lambda: (kv.at[0, c, y], y_far)) if P2_DIRECT
            else (lambda: (kv.at[0, c, y_lo, pl.ds(0, 2)], y_up)),
            lambda: (kv.at[0, c, y_hi, pl.ds(2, 2)], y_down),
            lambda: (kv.at[1, c, y, x], y_up),
            lambda: (kv.at[1, c, y, x], y_down),
            (lambda: (kv.at[1, c, y, x], y_far)) if P1_DIRECT
            else (lambda: (kv.at[1, c, y_lo, x, 0], y_up)),
            lambda: (kv.at[1, c, y_hi, x, 1], y_down),
            lambda: (kv.at[1, c, :, x], x_up),
            lambda: (kv.at[1, c, :, x], x_down),
            (lambda: (kv.at[1, c, :, x], x_far)) if P2_DIRECT
            else (lambda: (kv.at[1, c, pl.ds(0, 2), x_lo], x_up)),
            lambda: (kv.at[1, c, pl.ds(2, 2), x_hi], x_down),
        ]
        if number < 25:
            place, target = places[number]()
            source = place
        else:
            rest = pl.ds(pl.multiple_of((c - NC // 2) * R, R), R)
            source, place, target = q_away.at[:, rest], q_here.at[0, :, rest], partner
        return pltpu.make_async_remote_copy(
            src_ref=source, dst_ref=place, send_sem=c_send.at[c, number], recv_sem=c_recv.at[c, number],
            device_id=target, device_id_type=MESH,
        )

    def start(numbers, c):
        for number in numbers:
            copy_c(number, c).start()

    def arrive(numbers, c):
        for number in numbers:
            copy_c(number, c).wait_recv()

    def rotate(field, cos_rows, sin_rows):
        return field * cos_rows + pltpu.roll(field, HEAD_DIM // 2, 1) * sin_rows

    def project(c):
        rows = pl.ds(pl.multiple_of(c * R, R), R)
        squares = jnp.zeros((R, 512), jnp.float32)
        for piece in range(8):
            values = gathered[piece, rows].astype(jnp.float32)
            squares = squares + values * values
        scale = lax.rsqrt(jnp.sum(squares, axis=1, keepdims=True) * (1.0 / WIDTH) + 1e-05)
        total = jnp.zeros((R, 768), jnp.float32)
        for piece in range(8):
            values = gathered[piece, rows].astype(jnp.float32)
            normed = (values * scale * gain[piece * 512:(piece + 1) * 512].astype(jnp.float32).reshape(1, 512)).astype(jnp.bfloat16)
            total = total + jnp.dot(
                normed, wqkv[piece * 512:(piece + 1) * 512, :], preferred_element_type=jnp.float32
            )
        cos_rows, sin_rows = cosine[rows], sine[rows]
        kv[0, c, y, x, z_lo] = rotate(total[:, 512:640], cos_rows, sin_rows).astype(jnp.bfloat16)
        kv[1, c, y, x, z_lo] = total[:, 640:768].astype(jnp.bfloat16)
        queries = [
            rotate(total[:, h * 128:(h + 1) * 128], cos_rows, sin_rows).astype(jnp.bfloat16) for h in range(4)
        ]

        @pl.when(c < NC // 2)
        def _():
            for h in range(4):
                q_here[1, h, rows] = queries[h]

        @pl.when(c >= NC // 2)
        def _():
            rest = pl.ds(pl.multiple_of((c - NC // 2) * R, R), R)
            for h in range(4):
                q_away[h, rest] = queries[h]

    top[...] = jnp.full(top.shape, -1e30, jnp.float32)
    denom[...] = jnp.zeros(denom.shape, jnp.float32)
    acc[...] = jnp.zeros(acc.shape, jnp.float32)
    factor_log = LOG2E / HEAD_DIM ** 0.5

    def fold(c, half, group, masked):
        keys = kv[0, c, group].reshape(CHUNK_KEYS, HEAD_DIM)
        values = kv[1, c, group].reshape(CHUNK_KEYS, HEAD_DIM)
        queries = q_here[half].reshape(4 * HALF, HEAD_DIM)
        scores = lax.dot_general(
            queries, keys, (((1,), (1,)), ((), ())), preferred_element_type=jnp.float32
        )
        if masked:
            row = lax.broadcasted_iota(jnp.int32, (4 * HALF, 1), 0) % HALF + (1 - half) * HALF
            column = lax.broadcasted_iota(jnp.int32, (1, CHUNK_KEYS), 1)
            block = (column // R) % 2 * 4 + column // (2 * R)
            key_row = (block - (z_lo * 4 + x)) * ROWS + c * R + column % R
            scores = jnp.where(key_row <= row, scores, -2e30)
        old = top[half]
        newest = jnp.maximum(old, jnp.max(scores, axis=1, keepdims=True))
        top[half] = newest
        shrink = jnp.exp2((old - newest) * factor_log)
        wide = jnp.concatenate([newest] * (CHUNK_KEYS // 128), axis=1)
        weights = jnp.exp2((scores - wide) * factor_log)
        part = weights[:, 0:128]
        for at in range(1, CHUNK_KEYS // 128):
            part = part + weights[:, at * 128:(at + 1) * 128]
        denom[half] = denom[half] * shrink + part
        acc[half] = acc[half] * shrink + jnp.dot(
            weights.astype(jnp.bfloat16), values, preferred_element_type=jnp.float32
        )

    def attend(c):
        groups_away = 3 - y

        def body(step, carry):
            half = (step >= groups_away).astype(jnp.int32)
            group = step - half * groups_away
            fold(c, half, group, False)
            return carry

        lax.fori_loop(0, 3, body, 0)

        def diagonal(half, carry):
            fold(c, half, jnp.where(half == 0, 3 - y, y), True)
            return carry

        lax.fori_loop(0, 2, diagonal, 0)

    own = (0, 1, 3, 2) if A_DIRECT else (0, 1, 2)
    if P2_DIRECT:
        spread, last = (13, 14, 15, 21, 22, 23), (13, 14, 15, 21, 22, 23)
    else:
        spread, last = (13, 14, 21, 22), (15, 16, 23, 24)
    if P1_DIRECT:
        near = (9, 10, 11, 17, 18, 19)
    else:
        near = (9, 10, 17, 18)

    for c in range(AHEAD):
        start(own, c)

    def during(t, lag):
        return (t >= lag) & (t < NC + lag)

    def tick(t, carry):
        if not P2_DIRECT:
            @pl.when(during(t, LAG_S4))
            def _():
                arrive((13, 14), t - LAG_S4)
                start((15, 16), t - LAG_S4)
                arrive((21, 22), t - LAG_S4)
                start((23, 24), t - LAG_S4)

        @pl.when(during(t, LAG_S3))
        def _():
            arrive(near if P1_DIRECT else (11, 12, 19, 20), t - LAG_S3)
            start(spread, t - LAG_S3)

        if not P1_DIRECT:
            @pl.when(during(t, LAG_S2))
            def _():
                arrive((9, 10), t - LAG_S2)
                start((11, 12), t - LAG_S2)
                arrive((17, 18), t - LAG_S2)
                start((19, 20), t - LAG_S2)

        @pl.when(during(t, LAG_S1))
        def _():
            arrive((8,), t - LAG_S1)
            start(near, t - LAG_S1)

        if not A_DIRECT:
            @pl.when(during(t, LAG_A3))
            def _():
                arrive((3, 4), t - LAG_A3)
                start((7,), t - LAG_A3)

        @pl.when(t < NC)
        def _():
            if A_DIRECT:
                arrive((0, 1, 3), t)
                start((5, 6, 7), t)
            else:
                arrive((0, 1), t)
                start((3, 4, 5, 6), t)

        @pl.when(t + AHEAD < NC)
        def _():
            start(own, t + AHEAD)

        @pl.when(t == LAG_P)
        def _():
            for copy in weights[:3]:
                copy.wait()

        @pl.when(during(t, LAG_P))
        def _():
            arrive((2, 5, 6, 7), t - LAG_P)
            project(t - LAG_P)
            start((8,), t - LAG_P)

        @pl.when((t >= NC // 2 + LAG_P) & (t < NC + LAG_P))
        def _():
            start((25,), t - LAG_P)

        @pl.when(t == LAG_ATT)
        def _():
            for c in range(NC // 2, NC):
                arrive((25,), c)

        @pl.when(t >= LAG_ATT)
        def _():
            arrive(last, t - LAG_ATT)
            attend(t - LAG_ATT)

        return carry

    lax.fori_loop(0, NC + LAG_ATT, tick, 0)

    for half in range(2):
        whole = acc[half] / jnp.sum(denom[half], axis=1, keepdims=True)
        for h in range(4):
            att[half * HALF:(half + 1) * HALF, h * 128:(h + 1) * 128] = whole[
                h * HALF:(h + 1) * HALF
            ].astype(jnp.bfloat16)
    weights[3].wait()

    def copy_d(number, u):
        return pltpu.make_async_remote_copy(
            **dict(zip(("src_ref", "dst_ref", "device_id"), (
                lambda: (term_away.at[u], term_in.at[u], sibling),
                lambda: (relay_out.at[0, u], relay_in.at[0, u], z_up),
                lambda: (relay_out.at[1, u], relay_in.at[1, u], z_down),
                lambda: (fin_out.at[0, u], fin_in.at[0, u], z_up),
                lambda: (fin_out.at[1, u], fin_in.at[1, u], z_down),
                lambda: (
                    back.at[pl.ds(pl.multiple_of(u * CR, CR), CR)],
                    out.at[pl.ds(pl.multiple_of(HALF + u * CR, CR), CR)],
                    partner,
                ),
            )[number]())),
            send_sem=d_send.at[u, number], recv_sem=d_recv.at[u, number], device_id_type=MESH,
        )

    def term(u, column):
        return jnp.dot(
            att[pl.ds(pl.multiple_of(u * CR, CR), CR)],
            wov[:, pl.ds(pl.multiple_of(column * 512, 512), 512)],
            preferred_element_type=jnp.float32,
        ).astype(jnp.bfloat16)

    def paired(u, at, rows):
        return term_own[u, at, rows].astype(jnp.float32) + term_in[u, at, rows].astype(jnp.float32)

    low, high = pl.ds(0, CR // 2), pl.ds(CR // 2, CR // 2)
    opposite, above, below = (z_hi + 2) % 4, (z_hi + 1) % 4, (z_hi + 3) % 4

    def out_tick(u, carry):
        @pl.when(u < ND)
        def _():
            for at in range(4):
                term_away[u, at] = term(u, at * 2 + 1 - core)
            copy_d(0, u).start()
            for at in range(4):
                term_own[u, at] = term(u, at * 2 + core)
            copy_d(0, u).wait_recv()
            relay_out[0, u] = paired(u, opposite, low).astype(jnp.bfloat16)
            copy_d(1, u).start()
            relay_out[1, u] = paired(u, opposite, high).astype(jnp.bfloat16)
            copy_d(2, u).start()

        @pl.when((u >= LAG_D3) & (u < ND + LAG_D3))
        def _():
            v = u - LAG_D3
            copy_d(1, v).wait_recv()
            fin_out[0, v, low] = (paired(v, above, low) + relay_in[0, v].astype(jnp.float32)).astype(jnp.bfloat16)
            fin_out[0, v, high] = paired(v, above, high).astype(jnp.bfloat16)
            copy_d(3, v).start()
            copy_d(2, v).wait_recv()
            fin_out[1, v, low] = paired(v, below, low).astype(jnp.bfloat16)
            fin_out[1, v, high] = (paired(v, below, high) + relay_in[1, v].astype(jnp.float32)).astype(jnp.bfloat16)
            copy_d(4, v).start()

        @pl.when(u >= LAG_D4)
        def _():
            v = u - LAG_D4
            copy_d(3, v).wait_recv()
            copy_d(4, v).wait_recv()
            whole = (
                paired(v, z_hi, pl.ds(0, CR)) + fin_in[0, v].astype(jnp.float32) + fin_in[1, v].astype(jnp.float32)
            ).astype(jnp.bfloat16)

            @pl.when(v < ND // 2)
            def _():
                back[pl.ds(pl.multiple_of(v * CR, CR), CR)] = whole
                copy_d(5, v).start()

            @pl.when(v >= ND // 2)
            def _():
                out[pl.ds(pl.multiple_of(v * CR - HALF, CR), CR)] = whole

        return carry

    lax.fori_loop(0, ND + LAG_D4, out_tick, 0)

    unused = ((4,) if A_DIRECT else ()) + ((12, 20) if P1_DIRECT else ()) + ((16, 24) if P2_DIRECT else ())

    def drain_c(c, carry):
        for number in range(25):
            if number not in unused:
                copy_c(number, c).wait_send()
        return carry

    def drain_q(c, carry):
        copy_c(25, c).wait_send()
        return carry

    def drain_d(u, carry):
        for number in range(5):
            copy_d(number, u).wait_send()
        return carry

    def drain_y(u, carry):
        copy_d(5, u).wait()
        return carry

    lax.fori_loop(0, NC, drain_c, 0)
    lax.fori_loop(NC // 2, NC, drain_q, 0)
    lax.fori_loop(0, ND, drain_d, 0)
    lax.fori_loop(0, ND // 2, drain_y, 0)


def body(tokens, norm_gain, w_query, w_key, w_value, w_output):
    half = HEAD_DIM // 2
    frequency = 500000.0 ** (-2.0 * jnp.arange(half, dtype=jnp.float32) / HEAD_DIM)
    positions = lax.axis_index("ctx") * ROWS + jnp.arange(ROWS, dtype=jnp.int32)
    angles = positions.astype(jnp.float32)[:, None] * frequency[None, :]
    cosine = jnp.cos(angles)
    sine = jnp.sin(angles)
    cosine = jnp.concatenate([cosine, cosine], axis=1)
    sine = jnp.concatenate([-sine, sine], axis=1)
    vmem = pl.BlockSpec(memory_space=pltpu.VMEM)
    hbm = pl.BlockSpec(memory_space=pl.ANY)
    bf16, f32 = jnp.bfloat16, jnp.float32
    return pl.pallas_call(
        sublayer,
        out_shape=jax.ShapeDtypeStruct((ROWS, 512), bf16),
        in_specs=[hbm] + [vmem] * 3 + [hbm] * 4,
        out_specs=vmem,
        scratch_shapes=[
            pltpu.VMEM((8, ROWS, 512), bf16),
            pltpu.VMEM((WIDTH, 768), bf16),
            pltpu.VMEM((512, WIDTH), bf16),
            pltpu.VMEM((2, NC, 4, 4, 2, R, HEAD_DIM), bf16),
            pltpu.VMEM((2, 4, HALF, HEAD_DIM), bf16),
            pltpu.VMEM((4, HALF, HEAD_DIM), bf16),
            pltpu.VMEM((2, 4 * HALF, 128), f32),
            pltpu.VMEM((2, 4 * HALF, 128), f32),
            pltpu.VMEM((2, 4 * HALF, HEAD_DIM), f32),
            pltpu.VMEM((ROWS, 512), bf16),
            pltpu.VMEM((ND, 4, CR, 512), bf16),
            pltpu.VMEM((ND, 4, CR, 512), bf16),
            pltpu.VMEM((ND, 4, CR, 512), bf16),
            pltpu.VMEM((2, ND, CR // 2, 512), bf16),
            pltpu.VMEM((2, ND, CR // 2, 512), bf16),
            pltpu.VMEM((2, ND, CR, 512), bf16),
            pltpu.VMEM((2, ND, CR, 512), bf16),
            pltpu.VMEM((HALF, 512), bf16),
            pltpu.SemaphoreType.DMA((5,)),
            pltpu.SemaphoreType.DMA((NC, NS)),
            pltpu.SemaphoreType.DMA((NC, NS)),
            pltpu.SemaphoreType.DMA((ND, MS)),
            pltpu.SemaphoreType.DMA((ND, MS)),
        ],
        compiler_params=pltpu.CompilerParams(
            collective_id=0, has_side_effects=True, vmem_limit_bytes=62 << 20
        ),
        cost_estimate=pl.CostEstimate(flops=6_000_000_000, bytes_accessed=12_000_000, transcendentals=6_000_000),
    )(tokens, norm_gain, cosine, sine, w_query, w_key, w_value, w_output)


def solution(mesh):
    placed = (P("ctx", "tp"), P(), P(None, "tp"), P(None, "tp"), P(None, "tp"), P("tp", None))
    return jax.shard_map(
        body, mesh=mesh, in_specs=placed, out_specs=P("ctx", "tp"), check_vma=False
    )
```
